512 devices in a mesh: depth: 32 (over x, z_hi, core), res: 16 (over z_lo, y).
Axes of the slice: x: 4, y: 8, z: 8 (z_hi: 4, z_lo: 2; z = z_hi * 2 + z_lo), core: 2. Of those that a mesh axis runs over, the one named last changes fastest.
Arguments:
- aligned_activations: bfloat16 [64, 1024, 64], P('depth', 'res'), may hold values from -6 to 6
- couple_offset: bfloat16 [8, 1024, 1024], P(None, ('res', 'depth')), may hold values from -320 to 320
- mapping_matrix: bfloat16 [64, 256], replicated, may hold values from -0.75 to 0.75
- final_matrix: bfloat16 [64, 64], replicated, may hold values from -0.75 to 0.75
- result_cotangent: bfloat16 [64, 1024, 64], P('depth', 'res'), may hold values from -6 to 6
Outputs:
- update: bfloat16 [64, 1024, 64], P('depth', 'res')
- d_msa: bfloat16 [64, 1024, 64], P('depth', 'res')
- d_bias: float32 [8, 1024, 1024], P(None, ('res', 'depth'))
The draws below stay inside these ranges and needn't reach their ends.
All inputs are finite; a program needn't handle non-finite values.
Results may differ from the reference program's by a relative error of at most 0.025.
Values may be sent and summed in bfloat16 or wider, within the bound.
No kernel may reach another device: no remote copies, remote signals or barrier semaphores. Data moves between devices by JAX's collectives and lax.ppermute only.
A program may use at most 64 MiB of HBM per device.

```python
import math
import jax
import jax.numpy as jnp
from jax import lax

FEATURE_SPAN = 64
ATTENDER_TALLY = 8
HEAD_SPAN = 8
LOCAL_ALIGNED = 2
ALIGNED_TALLY = 64
AMINO_TALLY = 1024


def peaked_rows(key_list, background):
    head_keys = jax.random.split(key_list[2], ATTENDER_TALLY)
    chosen = jax.vmap(lambda single: jax.random.permutation(single, AMINO_TALLY))(head_keys).astype(jnp.int32)
    column = jnp.arange(AMINO_TALLY, dtype=jnp.int32)
    peak_mask = column[None, None, :] == chosen[:, :, None]
    height = jax.random.uniform(key_list[3], (ATTENDER_TALLY, AMINO_TALLY, 1), jnp.float32, 7.6, 8.2)
    flat_rows = jax.random.randint(key_list[4], (ATTENDER_TALLY, AMINO_TALLY, 1), 0, 10) < 3
    lifted = jnp.where(flat_rows, 0.0, height)
    return background + jnp.where(peak_mask, lifted, 0.0)


def draw_couple_offset(key, part):
    key = jax.random.fold_in(key, 11)
    key_list = jax.random.split(key, 9)
    background = jnp.clip(jax.random.normal(key_list[0], (ATTENDER_TALLY, AMINO_TALLY, AMINO_TALLY), jnp.float32) * 0.5, -1.5, 1.5)
    shaped = peaked_rows(key_list, background)
    return shaped.astype(jnp.bfloat16)


def draw_mapping_matrix(key, part):
    key = jax.random.fold_in(key, 13)
    values = jnp.clip(jax.random.normal(key, (FEATURE_SPAN, 4 * FEATURE_SPAN), jnp.float32), -6.0, 6.0) * FEATURE_SPAN ** (-0.5)
    return values.astype(jnp.bfloat16)


def draw_result_cotangent(key, part):
    key = jax.random.fold_in(key, 17)
    second_key = jax.random.fold_in(key, 1)
    values = jnp.clip(jax.random.normal(second_key, (ALIGNED_TALLY, AMINO_TALLY, FEATURE_SPAN), jnp.float32), -6.0, 6.0)
    return values.astype(jnp.bfloat16)


def block_scale(key, shape, shards, least, high):
    level, own = 1.0, jax.random.fold_in(key, 6)
    for axis_at, blocks in shards:
        draws = jnp.exp(jax.random.uniform(jax.random.fold_in(own, axis_at), (blocks,), jnp.float32, least / len(shards), high / len(shards)))
        level = level * jnp.repeat(draws, shape[axis_at] // blocks).reshape([-1 if axis == axis_at else 1 for axis in range(len(shape))])
    return level


def normal_values(stream_key, shape, deviation, most, cuts=(), kind=jnp.bfloat16):
    level = block_scale(stream_key, shape, cuts, -0.22, 0.18) if cuts else 1.0
    drawn = jax.random.normal(stream_key, shape, jnp.float32) * deviation * level
    return jnp.minimum(jnp.maximum(drawn, -most), most).astype(kind)


def setup_inputs(seed: int = 0) -> dict:
    arg_keys = jax.random.split(jax.random.key(seed), 6)
    return {
        "aligned_activations": normal_values(arg_keys[0], (ALIGNED_TALLY, AMINO_TALLY, FEATURE_SPAN), 1.0, 6.0, ((0, 32), (1, 16))),
        "couple_offset": draw_couple_offset(jax.random.fold_in(arg_keys[5], 71), 0),
        "mapping_matrix": draw_mapping_matrix(jax.random.fold_in(arg_keys[5], 71), 0),
        "final_matrix": normal_values(arg_keys[3], (FEATURE_SPAN, FEATURE_SPAN), FEATURE_SPAN ** -0.5, 0.75),
        "result_cotangent": draw_result_cotangent(jax.random.fold_in(arg_keys[5], 71), 0),
    }


EPS = 1e-05

def centering_statistic(x):
    row_average = lax.optimization_barrier(jnp.mean(x, -1, keepdims=True))
    cent = x - row_average
    var = lax.optimization_barrier(jnp.mean(cent * cent, -1, keepdims=True))
    reciprocal_spread = lax.rsqrt(var + EPS)
    return (cent * reciprocal_spread, reciprocal_spread)

def sequence_pass(input_halfprecision, d_out, bias_f, mapping_matrix, final_matrix):
    logit_factor = 1.0 / math.sqrt(HEAD_SPAN)
    rescaled_source, reciprocal_spread = centering_statistic(input_halfprecision.astype(jnp.float32))
    mapped_splits = jnp.dot(rescaled_source.astype(jnp.bfloat16), mapping_matrix, preferred_element_type=jnp.float32)
    asker_vectors = (mapped_splits[:, :FEATURE_SPAN] * logit_factor).astype(jnp.bfloat16).astype(jnp.float32).reshape(AMINO_TALLY, ATTENDER_TALLY, HEAD_SPAN)
    lookup_vectors = mapped_splits[:, FEATURE_SPAN:2 * FEATURE_SPAN].astype(jnp.bfloat16).astype(jnp.float32).reshape(AMINO_TALLY, ATTENDER_TALLY, HEAD_SPAN)
    payload_vectors = mapped_splits[:, 2 * FEATURE_SPAN:3 * FEATURE_SPAN].astype(jnp.bfloat16).astype(jnp.float32).reshape(AMINO_TALLY, ATTENDER_TALLY, HEAD_SPAN)
    sigmoid_switch = jax.nn.sigmoid(mapped_splits[:, 3 * FEATURE_SPAN:])
    scores = jnp.einsum('ihd,jhd->hij', asker_vectors, lookup_vectors) + bias_f
    top = lax.optimization_barrier(jnp.max(scores, -1, keepdims=True))
    lse = top + jnp.log(lax.optimization_barrier(jnp.sum(jnp.exp(scores - top), -1, keepdims=True)))
    probs = jnp.exp(scores - lse)
    softmax_brain = lax.optimization_barrier(probs.astype(jnp.bfloat16)).astype(jnp.float32)
    attending_result = jnp.einsum('tnu,uto->nto', softmax_brain, payload_vectors).reshape(AMINO_TALLY, FEATURE_SPAN)
    gated = (sigmoid_switch * attending_result).astype(jnp.bfloat16)
    update = jnp.dot(gated, final_matrix, preferred_element_type=jnp.float32).astype(jnp.bfloat16)
    d_gated = jnp.dot(d_out, final_matrix.T, preferred_element_type=jnp.float32)
    d_attn = lax.optimization_barrier((d_gated * sigmoid_switch).astype(jnp.bfloat16)).astype(jnp.float32)
    d_gate = d_gated * attending_result * sigmoid_switch * (1.0 - sigmoid_switch)
    attending_per_split = d_attn.reshape(AMINO_TALLY, ATTENDER_TALLY, HEAD_SPAN)
    delta = lax.optimization_barrier(jnp.sum(attending_per_split * attending_result.reshape(AMINO_TALLY, ATTENDER_TALLY, HEAD_SPAN), -1)).T
    d_probs = jnp.einsum('ihd,jhd->hij', attending_per_split, payload_vectors)
    d_scores = probs * (d_probs - delta[:, :, None])
    cotangent_logits_brain = lax.optimization_barrier(d_scores.astype(jnp.bfloat16)).astype(jnp.float32)
    cotangent_asker = jnp.einsum('tnu,uto->nto', cotangent_logits_brain, lookup_vectors).reshape(AMINO_TALLY, FEATURE_SPAN) * logit_factor
    cotangent_keyside = jnp.einsum('wcs,cwf->swf', cotangent_logits_brain, asker_vectors).reshape(AMINO_TALLY, FEATURE_SPAN)
    cotangent_payload = jnp.einsum('wcs,cwf->swf', softmax_brain, attending_per_split).reshape(AMINO_TALLY, FEATURE_SPAN)
    d_proj = jnp.concatenate([cotangent_asker, cotangent_keyside, cotangent_payload, d_gate], -1).astype(jnp.bfloat16)
    normalized_gradient = jnp.dot(d_proj, mapping_matrix.T, preferred_element_type=jnp.float32)
    input_gradient = reciprocal_spread * (normalized_gradient - lax.optimization_barrier(jnp.mean(normalized_gradient, -1, keepdims=True)) - rescaled_source * lax.optimization_barrier(jnp.mean(normalized_gradient * rescaled_source, -1, keepdims=True)))
    return (update, input_gradient.astype(jnp.bfloat16), d_scores)

def reference(aligned_activations, couple_offset, mapping_matrix, final_matrix, result_cotangent):
    bias_f = couple_offset.astype(jnp.float32)
    aligned_slices = ALIGNED_TALLY // LOCAL_ALIGNED
    aligned_groupings = aligned_activations.reshape(aligned_slices, LOCAL_ALIGNED, AMINO_TALLY, FEATURE_SPAN)
    cotangent_groupings = result_cotangent.reshape(aligned_slices, LOCAL_ALIGNED, AMINO_TALLY, FEATURE_SPAN)

    def batch_body(accrued_sum_value, pieces):

        def seq_step(acc, item):
            update, input_gradient, d_scores = sequence_pass(item[0], item[1], bias_f, mapping_matrix, final_matrix)
            return (acc + d_scores, (update, input_gradient))
        start = jnp.zeros((ATTENDER_TALLY, AMINO_TALLY, AMINO_TALLY), jnp.float32)
        acc, outs = lax.scan(seq_step, start, pieces)
        rounded = lax.optimization_barrier(acc.astype(jnp.bfloat16)).astype(jnp.float32)
        return (accrued_sum_value + rounded, outs)
    accrued_sum_value, (block_increments, matrix_cotangents) = lax.scan(batch_body, jnp.zeros((ATTENDER_TALLY, AMINO_TALLY, AMINO_TALLY), jnp.float32), (aligned_groupings, cotangent_groupings))
    return (block_increments.reshape(ALIGNED_TALLY, AMINO_TALLY, FEATURE_SPAN), matrix_cotangents.reshape(ALIGNED_TALLY, AMINO_TALLY, FEATURE_SPAN), accrued_sum_value)
```

```python
import math

import jax
import jax.numpy as jnp
from jax import lax
from jax.experimental import pallas as pl
from jax.experimental.pallas import tpu as pltpu
from jax.sharding import Mesh, PartitionSpec as P

HEADS = 8
HEAD_DIM = 8
EPS = 1e-05
SCALE = 1.0 / math.sqrt(HEAD_DIM)

DEPTH = ("x", "zh", "core")
RES = ("zl", "y")
HEAD_AXES = ("zl", "zh")
KEY_AXES = ("y",)
ROW_AXES = ("x", "core")


def tdot(a, b, ca, cb):
    return lax.dot_general(a, b, (((ca,), (cb,)), ((), ())), preferred_element_type=jnp.float32)


def project_kernel(x_hbm, rc_hbm, wm_hbm, wf_hbm, bias_hbm, pack_ref, xhat_ref, rstd_ref, g_ref, dg_ref,
                   x_ref, rc_ref, wm_ref, wf_ref, bias_ref, sems):
    pairs = [(x_hbm, x_ref), (wm_hbm, wm_ref), (rc_hbm, rc_ref), (wf_hbm, wf_ref), (bias_hbm, bias_ref)]
    copies = [pltpu.make_async_copy(a, b, sems.at[i]) for i, (a, b) in enumerate(pairs)]
    for copy in copies:
        copy.start()
    for copy in copies:
        copy.wait()
    x = x_ref[...].astype(jnp.float32).T
    cent = x - jnp.mean(x, 0, keepdims=True)
    rstd = lax.rsqrt(jnp.mean(cent * cent, 0, keepdims=True) + EPS)
    xhat = cent * rstd
    proj = tdot(wm_ref[...], xhat.astype(jnp.bfloat16), 0, 0)
    g = jax.nn.sigmoid(proj[192:256])
    d_gated = tdot(wf_ref[...], rc_ref[...], 1, 1)
    d_attn = d_gated * g
    xhat_ref[...] = xhat
    rstd_ref[...] = jnp.broadcast_to(rstd, rstd_ref.shape)
    g_ref[...] = g
    dg_ref[...] = d_gated
    for h in range(HEADS):
        lo, hi = h * HEAD_DIM, (h + 1) * HEAD_DIM
        b = bias_ref[h].astype(jnp.float32)
        parts = [proj[lo:hi] * SCALE, d_attn[lo:hi], proj[64 + lo : 64 + hi], proj[128 + lo : 128 + hi]]
        parts += [b[r : r + 1, c * 128 : c * 128 + 128] for r in range(2) for c in range(8)]
        pack_ref[h] = jnp.concatenate(parts, 0).astype(jnp.bfloat16)


def attend_kernel(pack_ref, kv_ref, bias_in_ref, dkv_ref, oq_ref, db_ref, bias_ref, acc_ref, tmp_ref):
    for zl in range(2):
        for x in range(4):
            for zh in range(4):
                for core in range(2):
                    at = (zh * 2 + core) * 16
                    tmp_ref[at : at + 16] = bias_in_ref[x * 2 + core, zl * 4 + zh].astype(jnp.float32)
            for c in range(8):
                at = (zl * 4 + x) * 16
                bias_ref[at : at + 16, c * 128 : c * 128 + 128] = tmp_ref[pl.ds(c, 16, stride=8)]
    rows = lax.broadcasted_iota(jnp.int32, (16, 128), 0)
    first = rows < HEAD_DIM
    ones = jnp.ones((16, 1024), jnp.bfloat16)
    for dl in range(4):
        dkv_pair, out_pair = [], []
        for s in range(2):
            lanes = slice(s * 64, s * 64 + 64)
            kv = jnp.concatenate(
                [kv_ref[y, zl * 4 + dl][:, lanes] for zl in range(2) for y in range(8)], 1
            )
            qd = jnp.concatenate([pack_ref[zl * 4 + dl, 0:16][:, lanes] for zl in range(2)], 1)
            qd = qd.astype(jnp.float32)
            q = jnp.where(first, qd, 0.0).astype(jnp.bfloat16)
            d = jnp.where(first, 0.0, qd)
            d_bf = d.astype(jnp.bfloat16)
            scores = tdot(q, kv, 0, 0) + bias_ref[...]
            e = jnp.exp(scores - jnp.max(scores, 1, keepdims=True))
            p = e * (1.0 / jnp.sum(e, 1, keepdims=True))
            p_bf = p.astype(jnp.bfloat16)
            attn = tdot(kv, p_bf, 1, 1)
            delta = -jnp.sum(d * attn, 0, keepdims=True)
            hi = delta.astype(jnp.bfloat16).astype(jnp.float32)
            mid = (delta - hi).astype(jnp.bfloat16).astype(jnp.float32)
            low = delta - hi - mid
            tail = jnp.where(rows == 0, hi, jnp.where(rows == 1, mid, jnp.where(rows == 2, low, 0.0)))
            lhs = jnp.concatenate([d, tail], 0).astype(jnp.bfloat16)
            ds = p * tdot(lhs, jnp.concatenate([kv, ones], 0), 0, 0)
            ds_bf = ds.astype(jnp.bfloat16)
            if dl == 0 and s == 0:
                acc_ref[...] = ds
            else:
                acc_ref[...] += ds
            dq = tdot(kv, ds_bf, 1, 1)
            both = jnp.concatenate([ds_bf, p_bf], 0)
            dkv_pair.append(tdot(jnp.concatenate([q, d_bf], 1), both, 1, 0).astype(jnp.bfloat16))
            out_pair.append(jnp.where(first, dq, attn).astype(jnp.bfloat16))
        for zl in range(2):
            part = slice(zl * 64, zl * 64 + 64)
            oq_ref[zl * 4 + dl] = jnp.concatenate([o[:, part] for o in out_pair], 1)
            for y in range(8):
                r = zl * 8 + y
                part_y = slice(r * 64, r * 64 + 64)
                dkv_ref[y, zl * 4 + dl] = jnp.concatenate([o[:, part_y] for o in dkv_pair], 1)
    for zl in range(2):
        for x in range(4):
            for c in range(8):
                at = (zl * 4 + x) * 16
                tmp_ref[pl.ds(c, 16, stride=8)] = acc_ref[at : at + 16, c * 128 : c * 128 + 128]
            for zh in range(4):
                for core in range(2):
                    at = (zh * 2 + core) * 16
                    db_ref[x * 2 + core, zl * 4 + zh] = tmp_ref[at : at + 16].astype(jnp.bfloat16)


def total(ref, h):
    acc = ref[0, h].astype(jnp.float32)
    for i in range(1, 8):
        acc += ref[i, h].astype(jnp.float32)
    return acc.astype(jnp.bfloat16)


def sum_kernel(oq_ref, dkv_ref, db_ref, pack_ref):
    for h in range(HEADS):
        pack_ref[h, 0:16] = oq_ref[h]
        pack_ref[h, 16:32] = total(dkv_ref, h)
        pack_ref[h, 32:48] = total(db_ref, h)


def finish_kernel(pack_ref, xhat_ref, rstd_ref, g_ref, dg_ref, wm_ref, wf_ref, up_ref, dx_ref, db_ref):
    dq, dk, dv, attn = [], [], [], []
    for h in range(HEADS):
        own = pack_ref[h].astype(jnp.float32)
        dq.append(own[0:8] * SCALE)
        attn.append(own[8:16])
        dk.append(own[16:24])
        dv.append(own[24:32])
        for r in range(2):
            db_ref[h, r : r + 1] = jnp.concatenate(
                [own[32 + r * 8 + c : 33 + r * 8 + c] for c in range(8)], 1
            )
    attn = jnp.concatenate(attn, 0)
    g = g_ref[...]
    gated = (g * attn).astype(jnp.bfloat16)
    up_ref[...] = tdot(gated, wf_ref[...], 0, 0).astype(jnp.bfloat16)
    d_gate = dg_ref[...] * attn * g * (1.0 - g)
    d_proj = jnp.concatenate(dq + dk + dv + [d_gate], 0).astype(jnp.bfloat16)
    d_normed = tdot(wm_ref[...], d_proj, 1, 0)
    xhat = xhat_ref[...]
    dx = rstd_ref[0:1] * (
        d_normed
        - jnp.mean(d_normed, 0, keepdims=True)
        - xhat * jnp.mean(d_normed * xhat, 0, keepdims=True)
    )
    dx_ref[...] = dx.T.astype(jnp.bfloat16)


def call(kernel, outs, *args, scratch=(), space=pltpu.VMEM, limit=40):
    return pl.pallas_call(
        kernel,
        out_shape=outs,
        in_specs=[pl.BlockSpec(memory_space=space)] * len(args),
        out_specs=[pl.BlockSpec(memory_space=pltpu.VMEM)] * len(outs),
        scratch_shapes=list(scratch),
        compiler_params=pltpu.CompilerParams(vmem_limit_bytes=limit * 1024 * 1024),
    )(*args)


def shape(*dims, dtype=jnp.bfloat16):
    return jax.ShapeDtypeStruct(dims, dtype)


def exchange(a, axes):
    return lax.all_to_all(a, axes, 0, 0, tiled=True)


def spread(a):
    return jnp.broadcast_to(a[None], (8,) + a.shape)


def per_device(x, bias, wm, wf, rc):
    f32 = jnp.float32
    pack, xhat, rstd, g, d_gated = call(
        project_kernel,
        [shape(8, 48, 128), shape(64, 128, dtype=f32), shape(8, 128, dtype=f32),
         shape(64, 128, dtype=f32), shape(64, 128, dtype=f32)],
        x.reshape(128, 64), rc.reshape(128, 64), wm, wf, bias,
        scratch=[pltpu.VMEM((128, 64), jnp.bfloat16), pltpu.VMEM((128, 64), jnp.bfloat16),
                 pltpu.VMEM((64, 256), jnp.bfloat16), pltpu.VMEM((64, 64), jnp.bfloat16),
                 pltpu.VMEM((8, 2, 1024), jnp.bfloat16), pltpu.SemaphoreType.DMA((5,))],
        space=pltpu.HBM, limit=60,
    )
    pack = exchange(pack, HEAD_AXES)
    kv = exchange(spread(pack[:, 16:32]), KEY_AXES)
    bias_rows = exchange(spread(pack[:, 32:48]), ROW_AXES)
    dkv, oq, db = call(
        attend_kernel,
        [shape(8, 8, 16, 128), shape(8, 16, 128), shape(8, 8, 16, 128)],
        pack, kv, bias_rows,
        scratch=[pltpu.VMEM((128, 1024), f32), pltpu.VMEM((128, 1024), f32), pltpu.VMEM((128, 128), f32)],
    )
    dkv = exchange(dkv, KEY_AXES)
    db = exchange(db, ROW_AXES)
    (back,) = call(sum_kernel, [shape(8, 48, 128)], oq, dkv, db)
    back = exchange(back, HEAD_AXES)
    update, dx, d_bias = call(
        finish_kernel,
        [shape(128, 64), shape(128, 64), shape(8, 2, 1024, dtype=f32)],
        back, xhat, rstd, g, d_gated, wm, wf,
    )
    return update.reshape(2, 64, 64), dx.reshape(2, 64, 64), d_bias


def solution(mesh):
    fine = Mesh(mesh.devices.reshape(4, 4, 2, 2, 8), DEPTH + RES)
    tokens = P(DEPTH, RES, None)
    rows = P(None, RES + DEPTH, None)
    return jax.shard_map(
        per_device,
        mesh=fine,
        in_specs=(tokens, rows, P(), P(), tokens),
        out_specs=(tokens, tokens, rows),
        check_vma=False,
    )
```

```python
import math

import jax
import jax.numpy as jnp
from jax import lax
from jax.experimental import pallas as pl
from jax.experimental.pallas import tpu as pltpu
from jax.sharding import Mesh, PartitionSpec as P

HEADS = 8
HEAD_DIM = 8
EPS = 1e-05
SCALE = 1.0 / math.sqrt(HEAD_DIM)

DEPTH = ("x", "zh", "core")
RES = ("zl", "y")
HEAD_AXES = ("zl", "zh")
KEY_AXES = ("y",)


def tdot(a, b, ca, cb):
    return lax.dot_general(a, b, (((ca,), (cb,)), ((), ())), preferred_element_type=jnp.float32)


def project_kernel(x_hbm, rc_hbm, wm_hbm, wf_hbm, bias_hbm, pack_ref, xhat_ref, rstd_ref, g_ref, dg_ref,
                   x_ref, rc_ref, wm_ref, wf_ref, bias_ref, sems):
    pairs = [(x_hbm, x_ref), (wm_hbm, wm_ref), (rc_hbm, rc_ref), (wf_hbm, wf_ref), (bias_hbm, bias_ref)]
    copies = [pltpu.make_async_copy(a, b, sems.at[i]) for i, (a, b) in enumerate(pairs)]
    for copy in copies:
        copy.start()
    for copy in copies:
        copy.wait()
    x = x_ref[...].astype(jnp.float32).T
    cent = x - jnp.mean(x, 0, keepdims=True)
    rstd = lax.rsqrt(jnp.mean(cent * cent, 0, keepdims=True) + EPS)
    xhat = cent * rstd
    proj = tdot(wm_ref[...], xhat.astype(jnp.bfloat16), 0, 0)
    g = jax.nn.sigmoid(proj[192:256])
    d_gated = tdot(wf_ref[...], rc_ref[...], 1, 1)
    d_attn = d_gated * g
    xhat_ref[...] = xhat
    rstd_ref[...] = jnp.broadcast_to(rstd, rstd_ref.shape)
    g_ref[...] = g
    dg_ref[...] = d_gated
    for h in range(HEADS):
        lo, hi = h * HEAD_DIM, (h + 1) * HEAD_DIM
        b = bias_ref[h].astype(jnp.float32)
        parts = [proj[lo:hi] * SCALE, d_attn[lo:hi], proj[64 + lo : 64 + hi], proj[128 + lo : 128 + hi]]
        parts += [b[r : r + 1, c * 128 : c * 128 + 128] for r in range(2) for c in range(8)]
        pack_ref[h] = jnp.concatenate(parts, 0).astype(jnp.bfloat16)


def attend_kernel(*refs):
    pack_ref, kv_ref, own_bias, swap_bias = refs[:4]
    oq_ref, dkv_ref, keep_ref, give_ref = refs[4:8]
    wide_ref, bias_ref, acc_ref, tmp_ref = refs[8:]
    me_x, core = lax.axis_index("x"), lax.axis_index("core")
    for k in range(4):
        at = lax.rem(me_x + 4 - k, 4) * 2
        for h in range(8):
            wide_ref[at + core, h] = own_bias[k, h].astype(jnp.float32)
            wide_ref[at + 1 - core, h] = swap_bias[k, h].astype(jnp.float32)
    for zl in range(2):
        for x in range(4):
            for zh in range(4):
                for half in range(2):
                    at = (zh * 2 + half) * 16
                    tmp_ref[at : at + 16] = wide_ref[x * 2 + half, zl * 4 + zh]
            for c in range(8):
                at = (zl * 4 + x) * 16
                bias_ref[at : at + 16, c * 128 : c * 128 + 128] = tmp_ref[pl.ds(c, 16, stride=8)]
    rows = lax.broadcasted_iota(jnp.int32, (16, 128), 0)
    first = rows < HEAD_DIM
    ones = jnp.ones((16, 1024), jnp.bfloat16)
    for dl in range(4):
        dkv_pair, out_pair = [], []
        for s in range(2):
            lanes = slice(s * 64, s * 64 + 64)
            kv = jnp.concatenate(
                [kv_ref[y, zl * 4 + dl][:, lanes] for zl in range(2) for y in range(8)], 1
            )
            qd = jnp.concatenate([pack_ref[zl * 4 + dl, 0:16][:, lanes] for zl in range(2)], 1)
            qd = qd.astype(jnp.float32)
            q = jnp.where(first, qd, 0.0).astype(jnp.bfloat16)
            d = jnp.where(first, 0.0, qd)
            d_bf = d.astype(jnp.bfloat16)
            scores = tdot(q, kv, 0, 0) + bias_ref[...]
            e = jnp.exp(scores - jnp.max(scores, 1, keepdims=True))
            p = e * (1.0 / jnp.sum(e, 1, keepdims=True))
            p_bf = p.astype(jnp.bfloat16)
            attn = tdot(kv, p_bf, 1, 1)
            delta = -jnp.sum(d * attn, 0, keepdims=True)
            hi = delta.astype(jnp.bfloat16).astype(jnp.float32)
            mid = (delta - hi).astype(jnp.bfloat16).astype(jnp.float32)
            low = delta - hi - mid
            tail = jnp.where(rows == 0, hi, jnp.where(rows == 1, mid, jnp.where(rows == 2, low, 0.0)))
            lhs = jnp.concatenate([d, tail], 0).astype(jnp.bfloat16)
            ds = p * tdot(lhs, jnp.concatenate([kv, ones], 0), 0, 0)
            ds_bf = ds.astype(jnp.bfloat16)
            if dl == 0 and s == 0:
                acc_ref[...] = ds
            else:
                acc_ref[...] += ds
            dq = tdot(kv, ds_bf, 1, 1)
            both = jnp.concatenate([ds_bf, p_bf], 0)
            dkv_pair.append(tdot(jnp.concatenate([q, d_bf], 1), both, 1, 0).astype(jnp.bfloat16))
            out_pair.append(jnp.where(first, dq, attn).astype(jnp.bfloat16))
        for zl in range(2):
            part = slice(zl * 64, zl * 64 + 64)
            oq_ref[zl * 4 + dl] = jnp.concatenate([o[:, part] for o in out_pair], 1)
            for y in range(8):
                r = zl * 8 + y
                part_y = slice(r * 64, r * 64 + 64)
                dkv_ref[y, zl * 4 + dl] = jnp.concatenate([o[:, part_y] for o in dkv_pair], 1)
    for zl in range(2):
        for x in range(4):
            for c in range(8):
                at = (zl * 4 + x) * 16
                tmp_ref[pl.ds(c, 16, stride=8)] = acc_ref[at : at + 16, c * 128 : c * 128 + 128]
            for zh in range(4):
                for half in range(2):
                    at = (zh * 2 + half) * 16
                    wide_ref[x * 2 + half, zl * 4 + zh] = tmp_ref[at : at + 16]
    for k in range(4):
        to = lax.rem(me_x + k, 4) * 2
        for h in range(8):
            keep_ref[k, h] = wide_ref[to + core, h].astype(jnp.bfloat16)
            give_ref[k, h] = wide_ref[to + 1 - core, h].astype(jnp.bfloat16)


def join_kernel(keep_ref, got_ref, *out_refs):
    for k in range(4):
        for h in range(HEADS):
            both = keep_ref[k, h].astype(jnp.float32) + got_ref[k, h].astype(jnp.float32)
            out_refs[k][h] = both.astype(jnp.bfloat16)


def total(blocks):
    acc = blocks[0].astype(jnp.float32)
    for block in blocks[1:]:
        acc += block.astype(jnp.float32)
    return acc.astype(jnp.bfloat16)


def sum_kernel(*refs):
    oq_ref, dkv_ref, db_refs, pack_ref = refs[0], refs[1], refs[2:6], refs[6]
    for h in range(HEADS):
        pack_ref[h, 0:16] = oq_ref[h]
        pack_ref[h, 16:32] = total([dkv_ref[y, h] for y in range(8)])
        pack_ref[h, 32:48] = total([ref[h] for ref in db_refs])


def finish_kernel(pack_ref, xhat_ref, rstd_ref, g_ref, dg_ref, wm_ref, wf_ref, up_ref, dx_ref, db_ref):
    dq, dk, dv, attn = [], [], [], []
    for h in range(HEADS):
        own = pack_ref[h].astype(jnp.float32)
        dq.append(own[0:8] * SCALE)
        attn.append(own[8:16])
        dk.append(own[16:24])
        dv.append(own[24:32])
        for r in range(2):
            db_ref[h, r : r + 1] = jnp.concatenate(
                [own[32 + r * 8 + c : 33 + r * 8 + c] for c in range(8)], 1
            )
    attn = jnp.concatenate(attn, 0)
    g = g_ref[...]
    gated = (g * attn).astype(jnp.bfloat16)
    up_ref[...] = tdot(gated, wf_ref[...], 0, 0).astype(jnp.bfloat16)
    d_gate = dg_ref[...] * attn * g * (1.0 - g)
    d_proj = jnp.concatenate(dq + dk + dv + [d_gate], 0).astype(jnp.bfloat16)
    d_normed = tdot(wm_ref[...], d_proj, 1, 0)
    xhat = xhat_ref[...]
    dx = rstd_ref[0:1] * (
        d_normed
        - jnp.mean(d_normed, 0, keepdims=True)
        - xhat * jnp.mean(d_normed * xhat, 0, keepdims=True)
    )
    dx_ref[...] = dx.T.astype(jnp.bfloat16)


def call(kernel, outs, *args, scratch=(), space=pltpu.VMEM, limit=40):
    return pl.pallas_call(
        kernel,
        out_shape=outs,
        in_specs=[pl.BlockSpec(memory_space=space)] * len(args),
        out_specs=[pl.BlockSpec(memory_space=pltpu.VMEM)] * len(outs),
        scratch_shapes=list(scratch),
        compiler_params=pltpu.CompilerParams(vmem_limit_bytes=limit * 1024 * 1024),
    )(*args)


def shape(*dims, dtype=jnp.bfloat16):
    return jax.ShapeDtypeStruct(dims, dtype)


def exchange(a, axes):
    return lax.all_to_all(a, axes, 0, 0, tiled=True)


def shift_x(a, k):
    return lax.ppermute(a, "x", [(i, (i + k) % 4) for i in range(4)])


def swap_core(a):
    return lax.ppermute(a, "core", [(0, 1), (1, 0)])


def per_device(x, bias, wm, wf, rc):
    f32 = jnp.float32
    pack, xhat, rstd, g, d_gated = call(
        project_kernel,
        [shape(8, 48, 128), shape(64, 128, dtype=f32), shape(8, 128, dtype=f32),
         shape(64, 128, dtype=f32), shape(64, 128, dtype=f32)],
        x.reshape(128, 64), rc.reshape(128, 64), wm, wf, bias,
        scratch=[pltpu.VMEM((128, 64), jnp.bfloat16), pltpu.VMEM((128, 64), jnp.bfloat16),
                 pltpu.VMEM((64, 256), jnp.bfloat16), pltpu.VMEM((64, 64), jnp.bfloat16),
                 pltpu.VMEM((8, 2, 1024), jnp.bfloat16), pltpu.SemaphoreType.DMA((5,))],
        space=pltpu.HBM, limit=60,
    )
    pack = exchange(pack, HEAD_AXES)
    own = pack[:, 16:32]
    kv = exchange(jnp.broadcast_to(own[None], (8,) + own.shape), KEY_AXES)
    own = pack[:, 32:48]
    own_bias = jnp.stack([own] + [shift_x(own, k) for k in range(1, 4)])
    swap_bias = swap_core(own_bias)
    block, quad, octet = shape(8, 16, 128), shape(4, 8, 16, 128), shape(8, 8, 16, 128)
    oq, dkv, keep, give = call(
        attend_kernel,
        [block, octet, quad, quad],
        pack, kv, own_bias, swap_bias,
        scratch=[pltpu.VMEM((8, 8, 16, 128), f32), pltpu.VMEM((128, 1024), f32),
                 pltpu.VMEM((128, 1024), f32), pltpu.VMEM((128, 128), f32)],
    )
    dkv = exchange(dkv, KEY_AXES)
    db = call(join_kernel, [block] * 4, keep, swap_core(give))
    db = [db[0]] + [shift_x(db[k], k) for k in range(1, 4)]
    (back,) = call(sum_kernel, [shape(8, 48, 128)], oq, dkv, *db)
    back = exchange(back, HEAD_AXES)
    update, dx, d_bias = call(
        finish_kernel,
        [shape(128, 64), shape(128, 64), shape(8, 2, 1024, dtype=f32)],
        back, xhat, rstd, g, d_gated, wm, wf,
    )
    return update.reshape(2, 64, 64), dx.reshape(2, 64, 64), d_bias


def solution(mesh):
    fine = Mesh(mesh.devices.reshape(4, 4, 2, 2, 8), DEPTH + RES)
    tokens = P(DEPTH, RES, None)
    rows = P(None, RES + DEPTH, None)
    return jax.shard_map(
        per_device,
        mesh=fine,
        in_specs=(tokens, rows, P(), P(), tokens),
        out_specs=(tokens, tokens, rows),
        check_vma=False,
    )
```

```python
import math

import jax
import jax.numpy as jnp
from jax import lax
from jax.experimental import pallas as pl
from jax.experimental.pallas import tpu as pltpu
from jax.sharding import Mesh, PartitionSpec as P

HEADS = 8
HEAD_DIM = 8
EPS = 1e-05
SCALE = 1.0 / math.sqrt(HEAD_DIM)

DEPTH = ("x", "zh", "core")
RES = ("zl", "y")
HEAD_AXES = ("zl", "zh")
KEY_AXES = ("zl", "zh", "y")


def tdot(a, b, ca, cb):
    return lax.dot_general(a, b, (((ca,), (cb,)), ((), ())), preferred_element_type=jnp.float32)


def project_kernel(x_hbm, rc_hbm, wm_hbm, wf_hbm, bias_hbm, kv_ref, pack_ref, save_ref,
                   x_ref, rc_ref, wm_ref, wf_ref, bias_ref, sems):
    pairs = [(x_hbm, x_ref), (wm_hbm, wm_ref), (rc_hbm, rc_ref), (wf_hbm, wf_ref), (bias_hbm, bias_ref)]
    copies = [pltpu.make_async_copy(a, b, sems.at[i]) for i, (a, b) in enumerate(pairs)]
    for copy in copies:
        copy.start()
    for copy in copies:
        copy.wait()
    x = x_ref[...].astype(jnp.float32).T
    cent = x - jnp.mean(x, 0, keepdims=True)
    rstd = lax.rsqrt(jnp.mean(cent * cent, 0, keepdims=True) + EPS)
    xhat = cent * rstd
    proj = tdot(wm_ref[...], xhat.astype(jnp.bfloat16), 0, 0)
    g = jax.nn.sigmoid(proj[192:256])
    d_gated = tdot(wf_ref[...], rc_ref[...], 1, 1)
    d_attn = d_gated * g
    save_ref[...] = jnp.concatenate([xhat, g, d_gated, jnp.broadcast_to(rstd, (8, 128))], 0)
    for h in range(HEADS):
        lo, hi = h * HEAD_DIM, (h + 1) * HEAD_DIM
        b = bias_ref[h].astype(jnp.float32)
        kv = jnp.concatenate([proj[64 + lo : 64 + hi], proj[128 + lo : 128 + hi]], 0)
        kv = kv.astype(jnp.bfloat16)
        for y in range(8):
            kv_ref[h, y] = kv
        parts = [proj[lo:hi] * SCALE, d_attn[lo:hi]]
        parts += [b[r : r + 1, c * 128 : c * 128 + 128] for r in range(2) for c in range(8)]
        pack_ref[h] = jnp.concatenate(parts, 0).astype(jnp.bfloat16)


def attend_kernel(*refs):
    pack_ref, kv_ref, own_bias, swap_bias = refs[:4]
    oq_ref, dkv_ref, keep_ref, give_ref = refs[4:8]
    wide_ref, bias_ref, acc_ref, tmp_ref = refs[8:]
    me_x, core = lax.axis_index("x"), lax.axis_index("core")
    flip = me_x + 1 - 2 * lax.rem(me_x, 2)
    order = [me_x, flip, 3 - me_x, 3 - flip]
    for k in range(4):
        at = order[k] * 2
        for h in range(8):
            wide_ref[at + core, h] = own_bias[k, h].astype(jnp.float32)
            wide_ref[at + 1 - core, h] = swap_bias[k, h].astype(jnp.float32)
    for zl in range(2):
        for x in range(4):
            for zh in range(4):
                for half in range(2):
                    at = (zh * 2 + half) * 16
                    tmp_ref[at : at + 16] = wide_ref[x * 2 + half, zl * 4 + zh]
            for c in range(8):
                at = (zl * 4 + x) * 16
                bias_ref[at : at + 16, c * 128 : c * 128 + 128] = tmp_ref[pl.ds(c, 16, stride=8)]
    rows = lax.broadcasted_iota(jnp.int32, (16, 128), 0)
    first = rows < HEAD_DIM
    ones = jnp.ones((16, 1024), jnp.bfloat16)
    for dl in range(4):
        dkv_pair, out_pair = [], []
        for s in range(2):
            lanes = slice(s * 64, s * 64 + 64)
            kv = jnp.concatenate(
                [kv_ref[zl * 4 + dl, y][:, lanes] for zl in range(2) for y in range(8)], 1
            )
            qd = jnp.concatenate([pack_ref[zl * 4 + dl, 0:16][:, lanes] for zl in range(2)], 1)
            qd = qd.astype(jnp.float32)
            q = jnp.where(first, qd, 0.0).astype(jnp.bfloat16)
            d = jnp.where(first, 0.0, qd)
            d_bf = d.astype(jnp.bfloat16)
            scores = tdot(q, kv, 0, 0) + bias_ref[...]
            e = jnp.exp(scores - jnp.max(scores, 1, keepdims=True))
            p = e * (1.0 / jnp.sum(e, 1, keepdims=True))
            p_bf = p.astype(jnp.bfloat16)
            attn = tdot(kv, p_bf, 1, 1)
            delta = -jnp.sum(d * attn, 0, keepdims=True)
            hi = delta.astype(jnp.bfloat16).astype(jnp.float32)
            mid = (delta - hi).astype(jnp.bfloat16).astype(jnp.float32)
            low = delta - hi - mid
            tail = jnp.where(rows == 0, hi, jnp.where(rows == 1, mid, jnp.where(rows == 2, low, 0.0)))
            lhs = jnp.concatenate([d, tail], 0).astype(jnp.bfloat16)
            ds = p * tdot(lhs, jnp.concatenate([kv, ones], 0), 0, 0)
            ds_bf = ds.astype(jnp.bfloat16)
            if dl == 0 and s == 0:
                acc_ref[...] = ds
            else:
                acc_ref[...] += ds
            dq = tdot(kv, ds_bf, 1, 1)
            both = jnp.concatenate([ds_bf, p_bf], 0)
            dkv_pair.append(tdot(jnp.concatenate([q, d_bf], 1), both, 1, 0).astype(jnp.bfloat16))
            out_pair.append(jnp.where(first, dq, attn).astype(jnp.bfloat16))
        for zl in range(2):
            part = slice(zl * 64, zl * 64 + 64)
            oq_ref[zl * 4 + dl] = jnp.concatenate([o[:, part] for o in out_pair], 1)
            for y in range(8):
                r = zl * 8 + y
                part_y = slice(r * 64, r * 64 + 64)
                dkv_ref[zl * 4 + dl, y] = jnp.concatenate([o[:, part_y] for o in dkv_pair], 1)
    for zl in range(2):
        for x in range(4):
            for c in range(8):
                at = (zl * 4 + x) * 16
                tmp_ref[pl.ds(c, 16, stride=8)] = acc_ref[at : at + 16, c * 128 : c * 128 + 128]
            for zh in range(4):
                for half in range(2):
                    at = (zh * 2 + half) * 16
                    wide_ref[x * 2 + half, zl * 4 + zh] = tmp_ref[at : at + 16]
    for k in range(4):
        to = order[k] * 2
        for h in range(8):
            keep_ref[k, h] = wide_ref[to + core, h].astype(jnp.bfloat16)
            give_ref[k, h] = wide_ref[to + 1 - core, h].astype(jnp.bfloat16)


def join_kernel(keep_ref, got_ref, stay_ref, go_ref):
    half = stay_ref.shape[0]
    for k in range(2 * half):
        for h in range(HEADS):
            both = keep_ref[k, h].astype(jnp.float32) + got_ref[k, h].astype(jnp.float32)
            out_ref = stay_ref if k < half else go_ref
            out_ref[k % half, h] = both.astype(jnp.bfloat16)


def pack_kernel(oq_ref, stay_ref, got_ref, pack_ref):
    for h in range(HEADS):
        pack_ref[h, 0:16] = oq_ref[h]
        both = stay_ref[0, h].astype(jnp.float32) + got_ref[0, h].astype(jnp.float32)
        pack_ref[h, 16:32] = both.astype(jnp.bfloat16)


def finish_kernel(pack_ref, dkv_ref, save_ref, wm_ref, wf_ref, up_ref, dx_ref, db_ref):
    dq, dk, dv, attn = [], [], [], []
    for h in range(HEADS):
        own = pack_ref[h].astype(jnp.float32)
        dq.append(own[0:8] * SCALE)
        attn.append(own[8:16])
        total = dkv_ref[h, 0].astype(jnp.float32)
        for y in range(1, 8):
            total += dkv_ref[h, y].astype(jnp.float32)
        dk.append(total[0:8])
        dv.append(total[8:16])
        for r in range(2):
            db_ref[h, r : r + 1] = jnp.concatenate(
                [own[16 + r * 8 + c : 17 + r * 8 + c] for c in range(8)], 1
            )
    attn = jnp.concatenate(attn, 0)
    xhat, g, d_gated, rstd = save_ref[0:64], save_ref[64:128], save_ref[128:192], save_ref[192:193]
    gated = (g * attn).astype(jnp.bfloat16)
    up_ref[...] = tdot(gated, wf_ref[...], 0, 0).astype(jnp.bfloat16)
    d_gate = d_gated * attn * g * (1.0 - g)
    d_proj = jnp.concatenate(dq + dk + dv + [d_gate], 0).astype(jnp.bfloat16)
    d_normed = tdot(wm_ref[...], d_proj, 1, 0)
    dx = rstd * (
        d_normed
        - jnp.mean(d_normed, 0, keepdims=True)
        - xhat * jnp.mean(d_normed * xhat, 0, keepdims=True)
    )
    dx_ref[...] = dx.T.astype(jnp.bfloat16)


def call(kernel, outs, *args, scratch=(), space=pltpu.VMEM, limit=40):
    return pl.pallas_call(
        kernel,
        out_shape=outs,
        in_specs=[pl.BlockSpec(memory_space=space)] * len(args),
        out_specs=[pl.BlockSpec(memory_space=pltpu.VMEM)] * len(outs),
        scratch_shapes=list(scratch),
        compiler_params=pltpu.CompilerParams(vmem_limit_bytes=limit * 1024 * 1024),
    )(*args)


def shape(*dims, dtype=jnp.bfloat16):
    return jax.ShapeDtypeStruct(dims, dtype)


def exchange(a, axes):
    return lax.all_to_all(a, axes, 0, 0, tiled=True)


def swap(a, axis, pairs):
    return lax.ppermute(a, axis, pairs + [(j, i) for i, j in pairs])


def swap_near(a):
    return swap(a, "x", [(0, 1), (2, 3)])


def swap_far(a):
    return swap(a, "x", [(0, 3), (1, 2)])


def swap_core(a):
    return swap(a, "core", [(0, 1)])


def per_device(x, bias, wm, wf, rc):
    f32 = jnp.float32
    kv, pack, saved = call(
        project_kernel,
        [shape(8, 8, 16, 128), shape(8, 32, 128), shape(200, 128, dtype=f32)],
        x.reshape(128, 64), rc.reshape(128, 64), wm, wf, bias,
        scratch=[pltpu.VMEM((128, 64), jnp.bfloat16), pltpu.VMEM((128, 64), jnp.bfloat16),
                 pltpu.VMEM((64, 256), jnp.bfloat16), pltpu.VMEM((64, 64), jnp.bfloat16),
                 pltpu.VMEM((8, 2, 1024), jnp.bfloat16), pltpu.SemaphoreType.DMA((5,))],
        space=pltpu.HBM, limit=60,
    )
    pack = exchange(pack, HEAD_AXES)
    kv, pack = lax.optimization_barrier((kv, pack))
    kv = exchange(kv.reshape(64, 16, 128), KEY_AXES).reshape(8, 8, 16, 128)
    own = pack[None, :, 16:32]
    own = jnp.concatenate([own, swap_near(own)])
    own = jnp.concatenate([own, swap_far(own)])
    sibling = swap_core(own)
    pair, quad, octet = shape(2, 8, 16, 128), shape(4, 8, 16, 128), shape(8, 8, 16, 128)
    oq, dkv, keep, give = call(
        attend_kernel,
        [shape(8, 16, 128), octet, quad, quad],
        pack, kv, own, sibling,
        scratch=[pltpu.VMEM((8, 8, 16, 128), f32), pltpu.VMEM((128, 1024), f32),
                 pltpu.VMEM((128, 1024), f32), pltpu.VMEM((128, 128), f32)],
    )
    dkv = exchange(dkv.reshape(64, 16, 128), KEY_AXES).reshape(8, 8, 16, 128)
    stay, go = call(join_kernel, [pair] * 2, keep, swap_core(give))
    stay, go = call(join_kernel, [shape(1, 8, 16, 128)] * 2, stay, swap_far(go))
    (back,) = call(pack_kernel, [shape(8, 32, 128)], oq, stay, swap_near(go))
    back = exchange(back, HEAD_AXES)
    update, dx, d_bias = call(
        finish_kernel,
        [shape(128, 64), shape(128, 64), shape(8, 2, 1024, dtype=f32)],
        back, dkv, saved, wm, wf,
    )
    return update.reshape(2, 64, 64), dx.reshape(2, 64, 64), d_bias


def solution(mesh):
    fine = Mesh(mesh.devices.reshape(4, 4, 2, 2, 8), DEPTH + RES)
    tokens = P(DEPTH, RES, None)
    rows = P(None, RES + DEPTH, None)
    return jax.shard_map(
        per_device,
        mesh=fine,
        in_specs=(tokens, rows, P(), P(), tokens),
        out_specs=(tokens, tokens, rows),
        check_vma=False,
    )
```

```python
import math

import jax
import jax.numpy as jnp
from jax import lax
from jax.experimental import pallas as pl
from jax.experimental.pallas import tpu as pltpu
from jax.sharding import Mesh, PartitionSpec as P

HEADS = 8
HEAD_DIM = 8
EPS = 1e-05
SCALE = 1.0 / math.sqrt(HEAD_DIM)

DEPTH = ("x", "zh", "core")
RES = ("zl", "y")
HEAD_AXES = ("zl", "zh")
KEY_AXES = ("y",)
ROW_AXES = ("x", "core")


def tdot(a, b, ca, cb):
    return lax.dot_general(a, b, (((ca,), (cb,)), ((), ())), preferred_element_type=jnp.float32)


def project_kernel(x_hbm, rc_hbm, wm_hbm, wf_hbm, bias_hbm, pack_ref, save_ref,
                   x_ref, rc_ref, wm_ref, wf_ref, bias_ref, sems):
    pairs = [(x_hbm, x_ref), (wm_hbm, wm_ref), (rc_hbm, rc_ref), (wf_hbm, wf_ref), (bias_hbm, bias_ref)]
    copies = [pltpu.make_async_copy(a, b, sems.at[i]) for i, (a, b) in enumerate(pairs)]
    for copy in copies:
        copy.start()
    for copy in copies:
        copy.wait()
    x = x_ref[...].astype(jnp.float32).T
    cent = x - jnp.mean(x, 0, keepdims=True)
    rstd = lax.rsqrt(jnp.mean(cent * cent, 0, keepdims=True) + EPS)
    xhat = cent * rstd
    proj = tdot(wm_ref[...], xhat.astype(jnp.bfloat16), 0, 0)
    g = jax.nn.sigmoid(proj[192:256])
    d_gated = tdot(wf_ref[...], rc_ref[...], 1, 1)
    d_attn = d_gated * g
    save_ref[...] = jnp.concatenate([xhat, g, d_gated, jnp.broadcast_to(rstd, (8, 128))], 0)
    for h in range(HEADS):
        lo, hi = h * HEAD_DIM, (h + 1) * HEAD_DIM
        b = bias_ref[h].astype(jnp.float32)
        parts = [proj[lo:hi] * SCALE, d_attn[lo:hi], proj[64 + lo : 64 + hi], proj[128 + lo : 128 + hi]]
        parts += [b[r : r + 1, c * 128 : c * 128 + 128] for r in range(2) for c in range(8)]
        pack_ref[h] = jnp.concatenate(parts, 0).astype(jnp.bfloat16)


def sequence_operands(pack_ref, kv_ref, dl, s):
    lanes = slice(s * 64, s * 64 + 64)
    kv = jnp.concatenate([kv_ref[y, zl * 4 + dl][:, lanes] for zl in range(2) for y in range(8)], 1)
    qd = jnp.concatenate([pack_ref[zl * 4 + dl, 0:16][:, lanes] for zl in range(2)], 1)
    qd = qd.astype(jnp.float32)
    first = lax.broadcasted_iota(jnp.int32, (16, 128), 0) < HEAD_DIM
    return kv, jnp.where(first, qd, 0.0), jnp.where(first, 0.0, qd), first


def score_kernel(pack_ref, kv_ref, own_ref, sibling_ref, p_ref, ds_ref, attn_ref, db_ref,
                 wide_ref, bias_ref, acc_ref, tmp_ref):
    core = lax.axis_index("core")
    for x in range(4):
        for h in range(8):
            wide_ref[x * 2 + core, h] = own_ref[x, h].astype(jnp.float32)
            wide_ref[x * 2 + 1 - core, h] = sibling_ref[x, h].astype(jnp.float32)
    for zl in range(2):
        for x in range(4):
            for zh in range(4):
                for half in range(2):
                    at = (zh * 2 + half) * 16
                    tmp_ref[at : at + 16] = wide_ref[x * 2 + half, zl * 4 + zh]
            for c in range(8):
                at = (zl * 4 + x) * 16
                bias_ref[at : at + 16, c * 128 : c * 128 + 128] = tmp_ref[pl.ds(c, 16, stride=8)]
    rows = lax.broadcasted_iota(jnp.int32, (16, 128), 0)
    ones = jnp.ones((16, 1024), jnp.bfloat16)
    for dl in range(4):
        for s in range(2):
            kv, q, d, first = sequence_operands(pack_ref, kv_ref, dl, s)
            scores = tdot(q.astype(jnp.bfloat16), kv, 0, 0) + bias_ref[...]
            e = jnp.exp(scores - jnp.max(scores, 1, keepdims=True))
            p = e * (1.0 / jnp.sum(e, 1, keepdims=True))
            p_bf = p.astype(jnp.bfloat16)
            attn = tdot(kv, p_bf, 1, 1)
            delta = -jnp.sum(d * attn, 0, keepdims=True)
            hi = delta.astype(jnp.bfloat16).astype(jnp.float32)
            mid = (delta - hi).astype(jnp.bfloat16).astype(jnp.float32)
            low = delta - hi - mid
            tail = jnp.where(rows == 0, hi, jnp.where(rows == 1, mid, jnp.where(rows == 2, low, 0.0)))
            lhs = jnp.concatenate([d, tail], 0).astype(jnp.bfloat16)
            ds = p * tdot(lhs, jnp.concatenate([kv, ones], 0), 0, 0)
            n = dl * 2 + s
            p_ref[n] = p_bf
            ds_ref[n] = ds.astype(jnp.bfloat16)
            attn_ref[n] = attn
            if n == 0:
                acc_ref[...] = ds
            else:
                acc_ref[...] += ds
    for zl in range(2):
        for x in range(4):
            for c in range(8):
                at = (zl * 4 + x) * 16
                tmp_ref[pl.ds(c, 16, stride=8)] = acc_ref[at : at + 16, c * 128 : c * 128 + 128]
            for zh in range(4):
                for half in range(2):
                    at = (zh * 2 + half) * 16
                    db_ref[x * 2 + half, zl * 4 + zh] = tmp_ref[at : at + 16].astype(jnp.bfloat16)


def gradient_kernel(pack_ref, kv_ref, p_ref, ds_ref, attn_ref, oq_ref, dkv_ref):
    for dl in range(4):
        dkv_pair, out_pair = [], []
        for s in range(2):
            kv, q, d, first = sequence_operands(pack_ref, kv_ref, dl, s)
            n = dl * 2 + s
            ds, p = ds_ref[n], p_ref[n]
            dq = tdot(kv, ds, 1, 1)
            lhs = jnp.concatenate([q, d], 1).astype(jnp.bfloat16)
            dkv = tdot(lhs, jnp.concatenate([ds, p], 0), 1, 0)
            dkv_pair.append(dkv.astype(jnp.bfloat16))
            out_pair.append(jnp.where(first, dq, attn_ref[n]).astype(jnp.bfloat16))
        for zl in range(2):
            part = slice(zl * 64, zl * 64 + 64)
            oq_ref[zl * 4 + dl] = jnp.concatenate([o[:, part] for o in out_pair], 1)
            for y in range(8):
                r = zl * 8 + y
                part_y = slice(r * 64, r * 64 + 64)
                dkv_ref[y, zl * 4 + dl] = jnp.concatenate([o[:, part_y] for o in dkv_pair], 1)


def total(ref, h):
    acc = ref[0, h].astype(jnp.float32)
    for i in range(1, 8):
        acc += ref[i, h].astype(jnp.float32)
    return acc.astype(jnp.bfloat16)


def sum_kernel(oq_ref, dkv_ref, db_ref, pack_ref):
    for h in range(HEADS):
        pack_ref[h, 0:16] = oq_ref[h]
        pack_ref[h, 16:32] = total(dkv_ref, h)
        pack_ref[h, 32:48] = total(db_ref, h)


def finish_kernel(pack_ref, save_ref, wm_ref, wf_ref, up_ref, dx_ref, db_ref):
    dq, dk, dv, attn = [], [], [], []
    for h in range(HEADS):
        own = pack_ref[h].astype(jnp.float32)
        dq.append(own[0:8] * SCALE)
        attn.append(own[8:16])
        dk.append(own[16:24])
        dv.append(own[24:32])
        for r in range(2):
            db_ref[h, r : r + 1] = jnp.concatenate(
                [own[32 + r * 8 + c : 33 + r * 8 + c] for c in range(8)], 1
            )
    attn = jnp.concatenate(attn, 0)
    xhat, g, d_gated, rstd = save_ref[0:64], save_ref[64:128], save_ref[128:192], save_ref[192:193]
    gated = (g * attn).astype(jnp.bfloat16)
    up_ref[...] = tdot(gated, wf_ref[...], 0, 0).astype(jnp.bfloat16)
    d_gate = d_gated * attn * g * (1.0 - g)
    d_proj = jnp.concatenate(dq + dk + dv + [d_gate], 0).astype(jnp.bfloat16)
    d_normed = tdot(wm_ref[...], d_proj, 1, 0)
    dx = rstd * (
        d_normed
        - jnp.mean(d_normed, 0, keepdims=True)
        - xhat * jnp.mean(d_normed * xhat, 0, keepdims=True)
    )
    dx_ref[...] = dx.T.astype(jnp.bfloat16)


def call(kernel, outs, *args, scratch=(), space=pltpu.VMEM, limit=40):
    return pl.pallas_call(
        kernel,
        out_shape=outs,
        in_specs=[pl.BlockSpec(memory_space=space)] * len(args),
        out_specs=[pl.BlockSpec(memory_space=pltpu.VMEM)] * len(outs),
        scratch_shapes=list(scratch),
        compiler_params=pltpu.CompilerParams(vmem_limit_bytes=limit * 1024 * 1024),
    )(*args)


def shape(*dims, dtype=jnp.bfloat16):
    return jax.ShapeDtypeStruct(dims, dtype)


def exchange(a, axes):
    return lax.all_to_all(a, axes, 0, 0, tiled=True)


def spread(a):
    return jnp.broadcast_to(a[None], (8,) + a.shape)


def per_device(x, bias, wm, wf, rc):
    f32 = jnp.float32
    pack, saved = call(
        project_kernel,
        [shape(8, 48, 128), shape(200, 128, dtype=f32)],
        x.reshape(128, 64), rc.reshape(128, 64), wm, wf, bias,
        scratch=[pltpu.VMEM((128, 64), jnp.bfloat16), pltpu.VMEM((128, 64), jnp.bfloat16),
                 pltpu.VMEM((64, 256), jnp.bfloat16), pltpu.VMEM((64, 64), jnp.bfloat16),
                 pltpu.VMEM((8, 2, 1024), jnp.bfloat16), pltpu.SemaphoreType.DMA((5,))],
        space=pltpu.HBM, limit=60,
    )
    pack = exchange(pack, HEAD_AXES)
    kv = exchange(spread(pack[:, 16:32]), KEY_AXES)
    own = lax.all_gather(pack[:, 32:48], "x")
    sibling = lax.ppermute(own, "core", [(0, 1), (1, 0)])
    octet, plane = shape(8, 8, 16, 128), pltpu.VMEM((128, 1024), f32)
    p, ds, attn, db = call(
        score_kernel,
        [shape(8, 128, 1024), shape(8, 128, 1024), shape(8, 16, 128, dtype=f32), octet],
        pack, kv, own, sibling,
        scratch=[pltpu.VMEM((8, 8, 16, 128), f32), plane, plane, pltpu.VMEM((128, 128), f32)],
    )
    db = exchange(db, ROW_AXES)
    oq, dkv = call(gradient_kernel, [shape(8, 16, 128), octet], pack, kv, p, ds, attn)
    dkv = exchange(dkv, KEY_AXES)
    (back,) = call(sum_kernel, [shape(8, 48, 128)], oq, dkv, db)
    back = exchange(back, HEAD_AXES)
    update, dx, d_bias = call(
        finish_kernel,
        [shape(128, 64), shape(128, 64), shape(8, 2, 1024, dtype=f32)],
        back, saved, wm, wf,
    )
    return update.reshape(2, 64, 64), dx.reshape(2, 64, 64), d_bias


def solution(mesh):
    fine = Mesh(mesh.devices.reshape(4, 4, 2, 2, 8), DEPTH + RES)
    tokens = P(DEPTH, RES, None)
    rows = P(None, RES + DEPTH, None)
    return jax.shard_map(
        per_device,
        mesh=fine,
        in_specs=(tokens, rows, P(), P(), tokens),
        out_specs=(tokens, tokens, rows),
        check_vma=False,
    )
```

```python
import math

import jax
import jax.numpy as jnp
from jax import lax
from jax.experimental import pallas as pl
from jax.experimental.pallas import tpu as pltpu
from jax.sharding import Mesh, PartitionSpec as P

HEADS = 8
HEAD_DIM = 8
EPS = 1e-05
SCALE = 1.0 / math.sqrt(HEAD_DIM)

DEPTH = ("x", "zh", "core")
RES = ("zl", "y")
HEAD_AXES = ("zl", "zh")
KEY_AXES = ("y",)
ROW_AXES = ("x", "core")
BLOCK = 32


def tdot(a, b, ca, cb):
    return lax.dot_general(a, b, (((ca,), (cb,)), ((), ())), preferred_element_type=jnp.float32)


def project_kernel(x_hbm, rc_hbm, wm_hbm, wf_hbm, bias_hbm, pack_ref, save_ref,
                   x_ref, rc_ref, wm_ref, wf_ref, bias_ref, sems):
    pairs = [(x_hbm, x_ref), (wm_hbm, wm_ref), (rc_hbm, rc_ref), (wf_hbm, wf_ref), (bias_hbm, bias_ref)]
    copies = [pltpu.make_async_copy(a, b, sems.at[i]) for i, (a, b) in enumerate(pairs)]
    for copy in copies:
        copy.start()
    for copy in copies:
        copy.wait()
    x = x_ref[...].astype(jnp.float32).T
    cent = x - jnp.mean(x, 0, keepdims=True)
    rstd = lax.rsqrt(jnp.mean(cent * cent, 0, keepdims=True) + EPS)
    xhat = cent * rstd
    proj = tdot(wm_ref[...], xhat.astype(jnp.bfloat16), 0, 0)
    g = jax.nn.sigmoid(proj[192:256])
    d_gated = tdot(wf_ref[...], rc_ref[...], 1, 1)
    d_attn = d_gated * g
    save_ref[...] = jnp.concatenate([xhat, g, d_gated, jnp.broadcast_to(rstd, (8, 128))], 0)
    for h in range(HEADS):
        lo, hi = h * HEAD_DIM, (h + 1) * HEAD_DIM
        b = bias_ref[h].astype(jnp.float32)
        parts = [proj[lo:hi] * SCALE, d_attn[lo:hi], proj[64 + lo : 64 + hi], proj[128 + lo : 128 + hi]]
        parts += [b[r : r + 1, c * 128 : c * 128 + 128] for r in range(2) for c in range(8)]
        pack_ref[h] = jnp.concatenate(parts, 0).astype(jnp.bfloat16)


def attend_kernel(pack_ref, kv_ref, own_ref, sibling_ref, dkv_ref, oq_ref, db_ref,
                  wide_ref, bias_ref, acc_ref, tmp_ref, pair_ref):
    me_x, core = lax.axis_index("x"), lax.axis_index("core")
    for k in range(4):
        at = lax.rem(me_x + 4 - k, 4) * 2
        for h in range(8):
            wide_ref[at + core, h] = own_ref[k, h].astype(jnp.float32)
            wide_ref[at + 1 - core, h] = sibling_ref[k, h].astype(jnp.float32)
    for zl in range(2):
        for x in range(4):
            for zh in range(4):
                for half in range(2):
                    at = (zh * 2 + half) * 16
                    tmp_ref[at : at + 16] = wide_ref[x * 2 + half, zl * 4 + zh]
            for c in range(8):
                at = (zl * 4 + x) * 16
                bias_ref[at : at + 16, c * 128 : c * 128 + 128] = tmp_ref[pl.ds(c, 16, stride=8)]
    upper = lax.broadcasted_iota(jnp.int32, (16, 128), 0) < HEAD_DIM
    left = lax.broadcasted_iota(jnp.int32, (128, 16), 1) < HEAD_DIM
    for dl in range(4):
        dkv_pair, out_pair = [], []
        for s in range(2):
            n = dl * 2 + s
            lanes = slice(s * 64, s * 64 + 64)
            kv = jnp.concatenate(
                [kv_ref[y, zl * 4 + dl][:, lanes] for zl in range(2) for y in range(8)], 1
            )
            qd = jnp.concatenate([pack_ref[zl * 4 + dl, 0:16][:, lanes] for zl in range(2)], 1)
            qd = qd.astype(jnp.float32)
            qd_rows = qd.T
            q_rows = jnp.where(left, qd_rows, 0.0).astype(jnp.bfloat16)
            d_rows = jnp.where(left, 0.0, qd_rows)
            d_bf = d_rows.astype(jnp.bfloat16)
            out_rows = []
            for at in range(0, 128, BLOCK):
                block = slice(at, at + BLOCK)
                scores = tdot(q_rows[block], kv, 1, 0) + bias_ref[block]
                e = jnp.exp(scores - jnp.max(scores, 1, keepdims=True))
                p = e * (1.0 / jnp.sum(e, 1, keepdims=True))
                p_bf = p.astype(jnp.bfloat16)
                pair_ref[n % 2, 128 + at : 128 + at + BLOCK] = p_bf
                attn = tdot(p_bf, kv, 1, 1)
                delta = jnp.sum(d_rows[block] * attn, 1, keepdims=True)
                ds = p * (tdot(d_bf[block], kv, 1, 0) - delta)
                ds_bf = ds.astype(jnp.bfloat16)
                pair_ref[n % 2, block] = ds_bf
                if n == 0:
                    acc_ref[block] = ds
                else:
                    acc_ref[block] += ds
                dq = tdot(ds_bf, kv, 1, 1)
                out_rows.append(jnp.where(left[block], dq, attn))
            lhs = jnp.concatenate([jnp.where(upper, qd, 0.0), jnp.where(upper, 0.0, qd)], 1)
            dkv_pair.append(tdot(lhs.astype(jnp.bfloat16), pair_ref[n % 2], 1, 0).astype(jnp.bfloat16))
            out_pair.append(jnp.concatenate(out_rows, 0).T.astype(jnp.bfloat16))
        for zl in range(2):
            part = slice(zl * 64, zl * 64 + 64)
            oq_ref[zl * 4 + dl] = jnp.concatenate([o[:, part] for o in out_pair], 1)
            for y in range(8):
                r = zl * 8 + y
                part_y = slice(r * 64, r * 64 + 64)
                dkv_ref[y, zl * 4 + dl] = jnp.concatenate([o[:, part_y] for o in dkv_pair], 1)
    for zl in range(2):
        for x in range(4):
            for c in range(8):
                at = (zl * 4 + x) * 16
                tmp_ref[pl.ds(c, 16, stride=8)] = acc_ref[at : at + 16, c * 128 : c * 128 + 128]
            for zh in range(4):
                for half in range(2):
                    at = (zh * 2 + half) * 16
                    db_ref[x * 2 + half, zl * 4 + zh] = tmp_ref[at : at + 16].astype(jnp.bfloat16)


def total(blocks):
    acc = blocks[0].astype(jnp.float32)
    for block in blocks[1:]:
        acc += block.astype(jnp.float32)
    return acc.astype(jnp.bfloat16)


def sum_kernel(oq_ref, dkv_ref, db_ref, pack_ref):
    for h in range(HEADS):
        pack_ref[h, 0:16] = oq_ref[h]
        pack_ref[h, 16:32] = total([dkv_ref[i, h] for i in range(8)])
        pack_ref[h, 32:48] = total([db_ref[i, h] for i in range(8)])


def finish_kernel(pack_ref, save_ref, wm_ref, wf_ref, up_ref, dx_ref, db_ref):
    dq, dk, dv, attn = [], [], [], []
    for h in range(HEADS):
        own = pack_ref[h].astype(jnp.float32)
        dq.append(own[0:8] * SCALE)
        attn.append(own[8:16])
        dk.append(own[16:24])
        dv.append(own[24:32])
        for r in range(2):
            db_ref[h, r : r + 1] = jnp.concatenate(
                [own[32 + r * 8 + c : 33 + r * 8 + c] for c in range(8)], 1
            )
    attn = jnp.concatenate(attn, 0)
    xhat, g, d_gated, rstd = save_ref[0:64], save_ref[64:128], save_ref[128:192], save_ref[192:193]
    gated = (g * attn).astype(jnp.bfloat16)
    up_ref[...] = tdot(gated, wf_ref[...], 0, 0).astype(jnp.bfloat16)
    d_gate = d_gated * attn * g * (1.0 - g)
    d_proj = jnp.concatenate(dq + dk + dv + [d_gate], 0).astype(jnp.bfloat16)
    d_normed = tdot(wm_ref[...], d_proj, 1, 0)
    dx = rstd * (
        d_normed
        - jnp.mean(d_normed, 0, keepdims=True)
        - xhat * jnp.mean(d_normed * xhat, 0, keepdims=True)
    )
    dx_ref[...] = dx.T.astype(jnp.bfloat16)


def call(kernel, outs, *args, scratch=(), space=pltpu.VMEM, limit=40):
    return pl.pallas_call(
        kernel,
        out_shape=outs,
        in_specs=[pl.BlockSpec(memory_space=space)] * len(args),
        out_specs=[pl.BlockSpec(memory_space=pltpu.VMEM)] * len(outs),
        scratch_shapes=list(scratch),
        compiler_params=pltpu.CompilerParams(vmem_limit_bytes=limit * 1024 * 1024),
    )(*args)


def shape(*dims, dtype=jnp.bfloat16):
    return jax.ShapeDtypeStruct(dims, dtype)


def exchange(a, axes):
    return lax.all_to_all(a, axes, 0, 0, tiled=True)


def shift_x(a, k):
    return lax.ppermute(a, "x", [(i, (i + k) % 4) for i in range(4)])


def swap_core(a):
    return lax.ppermute(a, "core", [(0, 1), (1, 0)])


def per_device(x, bias, wm, wf, rc):
    f32 = jnp.float32
    pack, saved = call(
        project_kernel,
        [shape(8, 48, 128), shape(200, 128, dtype=f32)],
        x.reshape(128, 64), rc.reshape(128, 64), wm, wf, bias,
        scratch=[pltpu.VMEM((128, 64), jnp.bfloat16), pltpu.VMEM((128, 64), jnp.bfloat16),
                 pltpu.VMEM((64, 256), jnp.bfloat16), pltpu.VMEM((64, 64), jnp.bfloat16),
                 pltpu.VMEM((8, 2, 1024), jnp.bfloat16), pltpu.SemaphoreType.DMA((5,))],
        space=pltpu.HBM, limit=60,
    )
    pack = exchange(pack, HEAD_AXES)
    own = pack[:, 16:32]
    kv = exchange(jnp.broadcast_to(own[None], (8,) + own.shape), KEY_AXES)
    own = pack[:, 32:48]
    own_bias = jnp.stack([own] + [shift_x(own, k) for k in range(1, 4)])
    swap_bias = swap_core(own_bias)
    octet, plane = shape(8, 8, 16, 128), pltpu.VMEM((128, 1024), f32)
    dkv, oq, db = call(
        attend_kernel,
        [octet, shape(8, 16, 128), octet],
        pack, kv, own_bias, swap_bias,
        scratch=[pltpu.VMEM((8, 8, 16, 128), f32), plane, plane, pltpu.VMEM((128, 128), f32),
                 pltpu.VMEM((2, 256, 1024), jnp.bfloat16)],
    )
    db = exchange(db, ROW_AXES)
    dkv = exchange(dkv, KEY_AXES)
    (back,) = call(sum_kernel, [shape(8, 48, 128)], oq, dkv, db)
    back = exchange(back, HEAD_AXES)
    update, dx, d_bias = call(
        finish_kernel,
        [shape(128, 64), shape(128, 64), shape(8, 2, 1024, dtype=f32)],
        back, saved, wm, wf,
    )
    return update.reshape(2, 64, 64), dx.reshape(2, 64, 64), d_bias


def solution(mesh):
    fine = Mesh(mesh.devices.reshape(4, 4, 2, 2, 8), DEPTH + RES)
    tokens = P(DEPTH, RES, None)
    rows = P(None, RES + DEPTH, None)
    return jax.shard_map(
        per_device,
        mesh=fine,
        in_specs=(tokens, rows, P(), P(), tokens),
        out_specs=(tokens, tokens, rows),
        check_vma=False,
    )
```

```python
import math

import jax
import jax.numpy as jnp
from jax import lax
from jax.experimental import pallas as pl
from jax.experimental.pallas import tpu as pltpu
from jax.sharding import Mesh, PartitionSpec as P

HEADS = 8
HEAD_DIM = 8
EPS = 1e-05
SCALE = 1.0 / math.sqrt(HEAD_DIM)

DEPTH = ("x", "zh", "core")
RES = ("zl", "y")
HEAD_AXES = ("zl", "zh")
KEY_AXES = ("y",)


def tdot(a, b, ca, cb):
    return lax.dot_general(a, b, (((ca,), (cb,)), ((), ())), preferred_element_type=jnp.float32)


def project_kernel(x_hbm, rc_hbm, wm_hbm, wf_hbm, bias_hbm, pack_ref, save_ref,
                   x_ref, rc_ref, wm_ref, wf_ref, bias_ref, sems):
    pairs = [(x_hbm, x_ref), (wm_hbm, wm_ref), (rc_hbm, rc_ref), (wf_hbm, wf_ref), (bias_hbm, bias_ref)]
    copies = [pltpu.make_async_copy(a, b, sems.at[i]) for i, (a, b) in enumerate(pairs)]
    for copy in copies:
        copy.start()
    for copy in copies:
        copy.wait()
    x = x_ref[...].astype(jnp.float32).T
    cent = x - jnp.mean(x, 0, keepdims=True)
    rstd = lax.rsqrt(jnp.mean(cent * cent, 0, keepdims=True) + EPS)
    xhat = cent * rstd
    proj = tdot(wm_ref[...], xhat.astype(jnp.bfloat16), 0, 0)
    g = jax.nn.sigmoid(proj[192:256])
    d_gated = tdot(wf_ref[...], rc_ref[...], 1, 1)
    d_attn = d_gated * g
    save_ref[...] = jnp.concatenate([xhat, g, d_gated, jnp.broadcast_to(rstd, (8, 128))], 0)
    for h in range(HEADS):
        lo, hi = h * HEAD_DIM, (h + 1) * HEAD_DIM
        b = bias_ref[h].astype(jnp.float32)
        parts = [proj[lo:hi] * SCALE, d_attn[lo:hi], proj[64 + lo : 64 + hi], proj[128 + lo : 128 + hi]]
        parts += [b[r : r + 1, c * 128 : c * 128 + 128] for r in range(2) for c in range(8)]
        pack_ref[h] = jnp.concatenate(parts, 0).astype(jnp.bfloat16)


def attend_kernel(pack_ref, kv_in_ref, own_ref, sibling_ref, oq_ref, dkv_ref, keep_ref, give_ref,
                  wide_ref, bias_ref, acc_ref, tmp_ref, kv_ref, t_ref, pair_ref):
    me_x, core = lax.axis_index("x"), lax.axis_index("core")
    for k in range(4):
        at = lax.rem(me_x + 4 - k, 4) * 2
        for h in range(8):
            wide_ref[at + core, h] = own_ref[k, h].astype(jnp.float32)
            wide_ref[at + 1 - core, h] = sibling_ref[k, h].astype(jnp.float32)
    groups = [(zl, x) for zl in range(2) for x in range(4)]
    for i, (zl, x) in enumerate(groups):
        for zh in range(4):
            for half in range(2):
                at = (zh * 2 + half) * 16
                tmp_ref[i, at : at + 16] = wide_ref[x * 2 + half, zl * 4 + zh]
    for i in range(8):
        for c in range(8):
            bias_ref[i * 16 : i * 16 + 16, c * 128 : c * 128 + 128] = tmp_ref[i, pl.ds(c, 16, stride=8)]
    left = lax.broadcasted_iota(jnp.int32, (128, 16), 1) < HEAD_DIM
    blocks = [slice(at, at + 16) for at in range(0, 128, 16)]
    queries, cots, tops, sums, deltas, scaled, attns = [], [], [], [], [], [], []
    for n in range(8):
        dl, lanes = n // 2, slice(n % 2 * 64, n % 2 * 64 + 64)
        kv_ref[n] = jnp.concatenate(
            [kv_in_ref[y, zl * 4 + dl][:, lanes] for zl in range(2) for y in range(8)], 1
        )
        qd = jnp.concatenate([pack_ref[zl * 4 + dl, 0:16][:, lanes] for zl in range(2)], 1)
        rows = qd.astype(jnp.float32).T
        queries.append(jnp.where(left, rows, 0.0))
        cots.append(jnp.where(left, 0.0, rows))
    for n in range(8):
        scores = tdot(queries[n].astype(jnp.bfloat16), kv_ref[n], 1, 0)
        top = []
        for b in blocks:
            t = scores[b] + bias_ref[b]
            t_ref[n, b] = t
            top.append(jnp.max(t, 1, keepdims=True))
        tops.append(top)
    for n in range(8):
        total = []
        for i, b in enumerate(blocks):
            e = jnp.exp(t_ref[n, b] - tops[n][i])
            total.append(jnp.sum(e, 1, keepdims=True))
            pair_ref[n, 128 + i * 16 : 144 + i * 16] = e.astype(jnp.bfloat16)
        sums.append(jnp.concatenate(total, 0))
    for n in range(8):
        inverse = 1.0 / sums[n]
        attn = tdot(pair_ref[n, 128:256], kv_ref[n], 1, 1) * inverse
        d = (cots[n] * inverse).astype(jnp.bfloat16)
        scaled.append(d)
        attns.append(attn)
        deltas.append(jnp.sum(d.astype(jnp.float32) * attn, 1, keepdims=True))
    for n in range(8):
        dp = tdot(scaled[n], kv_ref[n], 1, 0)
        for i, b in enumerate(blocks):
            e = pair_ref[n, 128 + i * 16 : 144 + i * 16].astype(jnp.float32)
            ds = e * (dp[b] - deltas[n][b])
            pair_ref[n, b] = ds.astype(jnp.bfloat16)
            if n == 0:
                acc_ref[b] = ds
            else:
                acc_ref[b] += ds
    outs, grads = [], []
    for n in range(8):
        dq = tdot(pair_ref[n, 0:128], kv_ref[n], 1, 1)
        outs.append(jnp.where(left, dq, attns[n]).T.astype(jnp.bfloat16))
        lhs = jnp.concatenate([queries[n].T, scaled[n].astype(jnp.float32).T], 1)
        grads.append(tdot(lhs.astype(jnp.bfloat16), pair_ref[n], 1, 0).astype(jnp.bfloat16))
    for dl in range(4):
        for zl in range(2):
            part = slice(zl * 64, zl * 64 + 64)
            oq_ref[zl * 4 + dl] = jnp.concatenate([outs[dl * 2 + s][:, part] for s in range(2)], 1)
            for y in range(8):
                r = zl * 8 + y
                part_y = slice(r * 64, r * 64 + 64)
                dkv_ref[y, zl * 4 + dl] = jnp.concatenate(
                    [grads[dl * 2 + s][:, part_y] for s in range(2)], 1
                )
    for i in range(8):
        for c in range(8):
            tmp_ref[i, pl.ds(c, 16, stride=8)] = acc_ref[i * 16 : i * 16 + 16, c * 128 : c * 128 + 128]
    for i, (zl, x) in enumerate(groups):
        for zh in range(4):
            for half in range(2):
                at = (zh * 2 + half) * 16
                wide_ref[x * 2 + half, zl * 4 + zh] = tmp_ref[i, at : at + 16]
    for k in range(4):
        to = lax.rem(me_x + k, 4) * 2
        for h in range(8):
            keep_ref[k, h] = wide_ref[to + core, h].astype(jnp.bfloat16)
            give_ref[k, h] = wide_ref[to + 1 - core, h].astype(jnp.bfloat16)


def join_kernel(keep_ref, got_ref, *out_refs):
    for k in range(4):
        for h in range(HEADS):
            both = keep_ref[k, h].astype(jnp.float32) + got_ref[k, h].astype(jnp.float32)
            out_refs[k][h] = both.astype(jnp.bfloat16)


def total(blocks):
    acc = blocks[0].astype(jnp.float32)
    for block in blocks[1:]:
        acc += block.astype(jnp.float32)
    return acc.astype(jnp.bfloat16)


def sum_kernel(*refs):
    oq_ref, dkv_ref, db_refs, pack_ref = refs[0], refs[1], refs[2:6], refs[6]
    for h in range(HEADS):
        pack_ref[h, 0:16] = oq_ref[h]
        pack_ref[h, 16:32] = total([dkv_ref[y, h] for y in range(8)])
        pack_ref[h, 32:48] = total([ref[h] for ref in db_refs])


def finish_kernel(pack_ref, save_ref, wm_ref, wf_ref, up_ref, dx_ref, db_ref):
    dq, dk, dv, attn = [], [], [], []
    for h in range(HEADS):
        own = pack_ref[h].astype(jnp.float32)
        dq.append(own[0:8] * SCALE)
        attn.append(own[8:16])
        dk.append(own[16:24])
        dv.append(own[24:32])
        for r in range(2):
            db_ref[h, r : r + 1] = jnp.concatenate(
                [own[32 + r * 8 + c : 33 + r * 8 + c] for c in range(8)], 1
            )
    attn = jnp.concatenate(attn, 0)
    xhat, g, d_gated, rstd = save_ref[0:64], save_ref[64:128], save_ref[128:192], save_ref[192:193]
    gated = (g * attn).astype(jnp.bfloat16)
    up_ref[...] = tdot(gated, wf_ref[...], 0, 0).astype(jnp.bfloat16)
    d_gate = d_gated * attn * g * (1.0 - g)
    d_proj = jnp.concatenate(dq + dk + dv + [d_gate], 0).astype(jnp.bfloat16)
    d_normed = tdot(wm_ref[...], d_proj, 1, 0)
    dx = rstd * (
        d_normed
        - jnp.mean(d_normed, 0, keepdims=True)
        - xhat * jnp.mean(d_normed * xhat, 0, keepdims=True)
    )
    dx_ref[...] = dx.T.astype(jnp.bfloat16)


def call(kernel, outs, *args, scratch=(), space=pltpu.VMEM, limit=40):
    return pl.pallas_call(
        kernel,
        out_shape=outs,
        in_specs=[pl.BlockSpec(memory_space=space)] * len(args),
        out_specs=[pl.BlockSpec(memory_space=pltpu.VMEM)] * len(outs),
        scratch_shapes=list(scratch),
        compiler_params=pltpu.CompilerParams(vmem_limit_bytes=limit * 1024 * 1024),
    )(*args)


def shape(*dims, dtype=jnp.bfloat16):
    return jax.ShapeDtypeStruct(dims, dtype)


def exchange(a, axes):
    return lax.all_to_all(a, axes, 0, 0, tiled=True)


def shift_x(a, k):
    return lax.ppermute(a, "x", [(i, (i + k) % 4) for i in range(4)])


def swap_core(a):
    return lax.ppermute(a, "core", [(0, 1), (1, 0)])


def per_device(x, bias, wm, wf, rc):
    f32 = jnp.float32
    pack, saved = call(
        project_kernel,
        [shape(8, 48, 128), shape(200, 128, dtype=f32)],
        x.reshape(128, 64), rc.reshape(128, 64), wm, wf, bias,
        scratch=[pltpu.VMEM((128, 64), jnp.bfloat16), pltpu.VMEM((128, 64), jnp.bfloat16),
                 pltpu.VMEM((64, 256), jnp.bfloat16), pltpu.VMEM((64, 64), jnp.bfloat16),
                 pltpu.VMEM((8, 2, 1024), jnp.bfloat16), pltpu.SemaphoreType.DMA((5,))],
        space=pltpu.HBM, limit=60,
    )
    pack = exchange(pack, HEAD_AXES)
    own = pack[:, 16:32]
    kv = exchange(jnp.broadcast_to(own[None], (8,) + own.shape), KEY_AXES)
    own = pack[:, 32:48]
    own_bias = jnp.stack([own] + [shift_x(own, k) for k in range(1, 4)])
    swap_bias = swap_core(own_bias)
    block, quad, octet = shape(8, 16, 128), shape(4, 8, 16, 128), shape(8, 8, 16, 128)
    oq, dkv, keep, give = call(
        attend_kernel,
        [block, octet, quad, quad],
        pack, kv, own_bias, swap_bias,
        scratch=[pltpu.VMEM((8, 8, 16, 128), f32), pltpu.VMEM((128, 1024), f32),
                 pltpu.VMEM((128, 1024), f32), pltpu.VMEM((8, 128, 128), f32),
                 pltpu.VMEM((8, 16, 1024), jnp.bfloat16), pltpu.VMEM((8, 128, 1024), f32),
                 pltpu.VMEM((8, 256, 1024), jnp.bfloat16)],
    )
    dkv = exchange(dkv, KEY_AXES)
    db = call(join_kernel, [block] * 4, keep, swap_core(give))
    db = [db[0]] + [shift_x(db[k], k) for k in range(1, 4)]
    (back,) = call(sum_kernel, [shape(8, 48, 128)], oq, dkv, *db)
    back = exchange(back, HEAD_AXES)
    update, dx, d_bias = call(
        finish_kernel,
        [shape(128, 64), shape(128, 64), shape(8, 2, 1024, dtype=f32)],
        back, saved, wm, wf,
    )
    return update.reshape(2, 64, 64), dx.reshape(2, 64, 64), d_bias


def solution(mesh):
    fine = Mesh(mesh.devices.reshape(4, 4, 2, 2, 8), DEPTH + RES)
    tokens = P(DEPTH, RES, None)
    rows = P(None, RES + DEPTH, None)
    return jax.shard_map(
        per_device,
        mesh=fine,
        in_specs=(tokens, rows, P(), P(), tokens),
        out_specs=(tokens, tokens, rows),
        check_vma=False,
    )
```

```python
import math

import jax
import jax.numpy as jnp
from jax import lax
from jax.experimental import pallas as pl
from jax.experimental.pallas import tpu as pltpu
from jax.sharding import Mesh, PartitionSpec as P

HEADS = 8
HEAD_DIM = 8
EPS = 1e-05
SCALE = 1.0 / math.sqrt(HEAD_DIM)

DEPTH = ("x", "zh", "core")
RES = ("zl", "y")
HEAD_AXES = ("zl", "zh")
KEY_AXES = ("y",)


def tdot(a, b, ca, cb):
    return lax.dot_general(a, b, (((ca,), (cb,)), ((), ())), preferred_element_type=jnp.float32)


def project_kernel(x_hbm, rc_hbm, wm_hbm, wf_hbm, bias_hbm, pack_ref, save_ref,
                   x_ref, rc_ref, wm_ref, wf_ref, bias_ref, sems):
    pairs = [(x_hbm, x_ref), (wm_hbm, wm_ref), (rc_hbm, rc_ref), (wf_hbm, wf_ref), (bias_hbm, bias_ref)]
    copies = [pltpu.make_async_copy(a, b, sems.at[i]) for i, (a, b) in enumerate(pairs)]
    for copy in copies:
        copy.start()
    for copy in copies:
        copy.wait()
    x = x_ref[...].astype(jnp.float32).T
    cent = x - jnp.mean(x, 0, keepdims=True)
    rstd = lax.rsqrt(jnp.mean(cent * cent, 0, keepdims=True) + EPS)
    xhat = cent * rstd
    proj = tdot(wm_ref[...], xhat.astype(jnp.bfloat16), 0, 0)
    g = jax.nn.sigmoid(proj[192:256])
    d_gated = tdot(wf_ref[...], rc_ref[...], 1, 1)
    d_attn = d_gated * g
    save_ref[...] = jnp.concatenate([xhat, g, d_gated, jnp.broadcast_to(rstd, (8, 128))], 0)
    for h in range(HEADS):
        lo, hi = h * HEAD_DIM, (h + 1) * HEAD_DIM
        b = bias_ref[h].astype(jnp.float32)
        parts = [proj[lo:hi] * SCALE, d_attn[lo:hi], proj[64 + lo : 64 + hi], proj[128 + lo : 128 + hi]]
        parts += [b[r : r + 1, c * 128 : c * 128 + 128] for r in range(2) for c in range(8)]
        pack_ref[h] = jnp.concatenate(parts, 0).astype(jnp.bfloat16)


def attend_kernel(pack_ref, kv_in_ref, bias_in_ref, oq_ref, dkv_ref, keep_ref, give_ref,
                  wide_ref, bias_ref, acc_ref, tmp_ref, kv_ref, t_ref, pair_ref):
    core = lax.axis_index("core")
    for x in range(4):
        for h in range(8):
            wide_ref[x * 2 + core, h] = bias_in_ref[x, 0, h].astype(jnp.float32)
            wide_ref[x * 2 + 1 - core, h] = bias_in_ref[x, 1, h].astype(jnp.float32)
    groups = [(zl, x) for zl in range(2) for x in range(4)]
    for i, (zl, x) in enumerate(groups):
        for zh in range(4):
            for half in range(2):
                at = (zh * 2 + half) * 16
                tmp_ref[i, at : at + 16] = wide_ref[x * 2 + half, zl * 4 + zh]
    for i in range(8):
        for c in range(8):
            bias_ref[i * 16 : i * 16 + 16, c * 128 : c * 128 + 128] = tmp_ref[i, pl.ds(c, 16, stride=8)]
    left = lax.broadcasted_iota(jnp.int32, (128, 16), 1) < HEAD_DIM
    blocks = [slice(at, at + 16) for at in range(0, 128, 16)]
    queries, cots, tops, sums, deltas, scaled, attns = [], [], [], [], [], [], []
    for n in range(8):
        dl, lanes = n // 2, slice(n % 2 * 64, n % 2 * 64 + 64)
        kv_ref[n] = jnp.concatenate(
            [kv_in_ref[y, zl * 4 + dl][:, lanes] for zl in range(2) for y in range(8)], 1
        )
        qd = jnp.concatenate([pack_ref[zl * 4 + dl, 0:16][:, lanes] for zl in range(2)], 1)
        rows = qd.astype(jnp.float32).T
        queries.append(jnp.where(left, rows, 0.0))
        cots.append(jnp.where(left, 0.0, rows))
    for n in range(8):
        scores = tdot(queries[n].astype(jnp.bfloat16), kv_ref[n], 1, 0)
        top = []
        for b in blocks:
            t = scores[b] + bias_ref[b]
            t_ref[n, b] = t
            top.append(jnp.max(t, 1, keepdims=True))
        tops.append(top)
    for n in range(8):
        total = []
        for i, b in enumerate(blocks):
            e = jnp.exp(t_ref[n, b] - tops[n][i])
            total.append(jnp.sum(e, 1, keepdims=True))
            pair_ref[n, 128 + i * 16 : 144 + i * 16] = e.astype(jnp.bfloat16)
        sums.append(jnp.concatenate(total, 0))
    for n in range(8):
        inverse = 1.0 / sums[n]
        attn = tdot(pair_ref[n, 128:256], kv_ref[n], 1, 1) * inverse
        d = (cots[n] * inverse).astype(jnp.bfloat16)
        scaled.append(d)
        attns.append(attn)
        deltas.append(jnp.sum(d.astype(jnp.float32) * attn, 1, keepdims=True))
    for n in range(8):
        dp = tdot(scaled[n], kv_ref[n], 1, 0)
        for i, b in enumerate(blocks):
            e = pair_ref[n, 128 + i * 16 : 144 + i * 16].astype(jnp.float32)
            ds = e * (dp[b] - deltas[n][b])
            pair_ref[n, b] = ds.astype(jnp.bfloat16)
            if n == 0:
                acc_ref[b] = ds
            else:
                acc_ref[b] += ds
    outs, grads = [], []
    for n in range(8):
        dq = tdot(pair_ref[n, 0:128], kv_ref[n], 1, 1)
        outs.append(jnp.where(left, dq, attns[n]).T.astype(jnp.bfloat16))
        lhs = jnp.concatenate([queries[n].T, scaled[n].astype(jnp.float32).T], 1)
        grads.append(tdot(lhs.astype(jnp.bfloat16), pair_ref[n], 1, 0).astype(jnp.bfloat16))
    for dl in range(4):
        for zl in range(2):
            part = slice(zl * 64, zl * 64 + 64)
            oq_ref[zl * 4 + dl] = jnp.concatenate([outs[dl * 2 + s][:, part] for s in range(2)], 1)
            for y in range(8):
                r = zl * 8 + y
                part_y = slice(r * 64, r * 64 + 64)
                dkv_ref[y, zl * 4 + dl] = jnp.concatenate(
                    [grads[dl * 2 + s][:, part_y] for s in range(2)], 1
                )
    for i in range(8):
        for c in range(8):
            tmp_ref[i, pl.ds(c, 16, stride=8)] = acc_ref[i * 16 : i * 16 + 16, c * 128 : c * 128 + 128]
    for i, (zl, x) in enumerate(groups):
        for zh in range(4):
            for half in range(2):
                at = (zh * 2 + half) * 16
                wide_ref[x * 2 + half, zl * 4 + zh] = tmp_ref[i, at : at + 16]
    for x in range(4):
        for h in range(8):
            keep_ref[x, h] = wide_ref[x * 2 + core, h].astype(jnp.bfloat16)
            give_ref[x, h] = wide_ref[x * 2 + 1 - core, h].astype(jnp.bfloat16)


def join_kernel(keep_ref, got_ref, out_ref):
    for x in range(4):
        for h in range(HEADS):
            both = keep_ref[x, h].astype(jnp.float32) + got_ref[x, h].astype(jnp.float32)
            out_ref[x, h] = both.astype(jnp.bfloat16)


def total(blocks):
    acc = blocks[0].astype(jnp.float32)
    for block in blocks[1:]:
        acc += block.astype(jnp.float32)
    return acc.astype(jnp.bfloat16)


def sum_kernel(oq_ref, dkv_ref, db_ref, pack_ref):
    for h in range(HEADS):
        pack_ref[h, 0:16] = oq_ref[h]
        pack_ref[h, 16:32] = total([dkv_ref[y, h] for y in range(8)])
        pack_ref[h, 32:48] = total([db_ref[x, h] for x in range(4)])


def finish_kernel(pack_ref, save_ref, wm_ref, wf_ref, up_ref, dx_ref, db_ref):
    dq, dk, dv, attn = [], [], [], []
    for h in range(HEADS):
        own = pack_ref[h].astype(jnp.float32)
        dq.append(own[0:8] * SCALE)
        attn.append(own[8:16])
        dk.append(own[16:24])
        dv.append(own[24:32])
        for r in range(2):
            db_ref[h, r : r + 1] = jnp.concatenate(
                [own[32 + r * 8 + c : 33 + r * 8 + c] for c in range(8)], 1
            )
    attn = jnp.concatenate(attn, 0)
    xhat, g, d_gated, rstd = save_ref[0:64], save_ref[64:128], save_ref[128:192], save_ref[192:193]
    gated = (g * attn).astype(jnp.bfloat16)
    up_ref[...] = tdot(gated, wf_ref[...], 0, 0).astype(jnp.bfloat16)
    d_gate = d_gated * attn * g * (1.0 - g)
    d_proj = jnp.concatenate(dq + dk + dv + [d_gate], 0).astype(jnp.bfloat16)
    d_normed = tdot(wm_ref[...], d_proj, 1, 0)
    dx = rstd * (
        d_normed
        - jnp.mean(d_normed, 0, keepdims=True)
        - xhat * jnp.mean(d_normed * xhat, 0, keepdims=True)
    )
    dx_ref[...] = dx.T.astype(jnp.bfloat16)


def call(kernel, outs, *args, scratch=(), space=pltpu.VMEM, limit=40):
    return pl.pallas_call(
        kernel,
        out_shape=outs,
        in_specs=[pl.BlockSpec(memory_space=space)] * len(args),
        out_specs=[pl.BlockSpec(memory_space=pltpu.VMEM)] * len(outs),
        scratch_shapes=list(scratch),
        compiler_params=pltpu.CompilerParams(vmem_limit_bytes=limit * 1024 * 1024),
    )(*args)


def shape(*dims, dtype=jnp.bfloat16):
    return jax.ShapeDtypeStruct(dims, dtype)


def exchange(a, axes):
    return lax.all_to_all(a, axes, 0, 0, tiled=True)


def swap_core(a):
    return lax.ppermute(a, "core", [(0, 1), (1, 0)])


def per_device(x, bias, wm, wf, rc):
    f32 = jnp.float32
    pack, saved = call(
        project_kernel,
        [shape(8, 48, 128), shape(200, 128, dtype=f32)],
        x.reshape(128, 64), rc.reshape(128, 64), wm, wf, bias,
        scratch=[pltpu.VMEM((128, 64), jnp.bfloat16), pltpu.VMEM((128, 64), jnp.bfloat16),
                 pltpu.VMEM((64, 256), jnp.bfloat16), pltpu.VMEM((64, 64), jnp.bfloat16),
                 pltpu.VMEM((8, 2, 1024), jnp.bfloat16), pltpu.SemaphoreType.DMA((5,))],
        space=pltpu.HBM, limit=60,
    )
    pack = exchange(pack, HEAD_AXES)
    own = pack[:, 16:32]
    kv = exchange(jnp.broadcast_to(own[None], (8,) + own.shape), KEY_AXES)
    own = pack[:, 32:48]
    pair = jnp.stack([own, swap_core(own)])
    kv, pair = lax.optimization_barrier((kv, pair))
    bias_rows = exchange(jnp.broadcast_to(pair[None], (4,) + pair.shape), ("x",))
    block, quad, octet = shape(8, 16, 128), shape(4, 8, 16, 128), shape(8, 8, 16, 128)
    oq, dkv, keep, give = call(
        attend_kernel,
        [block, octet, quad, quad],
        pack, kv, bias_rows,
        scratch=[pltpu.VMEM((8, 8, 16, 128), f32), pltpu.VMEM((128, 1024), f32),
                 pltpu.VMEM((128, 1024), f32), pltpu.VMEM((8, 128, 128), f32),
                 pltpu.VMEM((8, 16, 1024), jnp.bfloat16), pltpu.VMEM((8, 128, 1024), f32),
                 pltpu.VMEM((8, 256, 1024), jnp.bfloat16)],
    )
    dkv = exchange(dkv, KEY_AXES)
    (db,) = call(join_kernel, [quad], keep, swap_core(give))
    dkv, db = lax.optimization_barrier((dkv, db))
    db = exchange(db, ("x",))
    (back,) = call(sum_kernel, [shape(8, 48, 128)], oq, dkv, db)
    back = exchange(back, HEAD_AXES)
    update, dx, d_bias = call(
        finish_kernel,
        [shape(128, 64), shape(128, 64), shape(8, 2, 1024, dtype=f32)],
        back, saved, wm, wf,
    )
    return update.reshape(2, 64, 64), dx.reshape(2, 64, 64), d_bias


def solution(mesh):
    fine = Mesh(mesh.devices.reshape(4, 4, 2, 2, 8), DEPTH + RES)
    tokens = P(DEPTH, RES, None)
    rows = P(None, RES + DEPTH, None)
    return jax.shard_map(
        per_device,
        mesh=fine,
        in_specs=(tokens, rows, P(), P(), tokens),
        out_specs=(tokens, tokens, rows),
        check_vma=False,
    )
```

```python
import math

import jax
import jax.numpy as jnp
from jax import lax
from jax.experimental import pallas as pl
from jax.experimental.pallas import tpu as pltpu
from jax.sharding import Mesh, PartitionSpec as P

HEADS = 8
HEAD_DIM = 8
EPS = 1e-05
SCALE = 1.0 / math.sqrt(HEAD_DIM)

DEPTH = ("x", "zh", "core")
RES = ("zl", "y")
HEAD_AXES = ("zl", "zh")
KEY_AXES = ("y",)


def tdot(a, b, ca, cb):
    return lax.dot_general(a, b, (((ca,), (cb,)), ((), ())), preferred_element_type=jnp.float32)


def project_kernel(x_hbm, rc_hbm, wm_hbm, wf_hbm, bias_hbm, pack_ref, save_ref,
                   x_ref, rc_ref, wm_ref, wf_ref, bias_ref, sems):
    pairs = [(x_hbm, x_ref), (wm_hbm, wm_ref), (rc_hbm, rc_ref), (wf_hbm, wf_ref), (bias_hbm, bias_ref)]
    copies = [pltpu.make_async_copy(a, b, sems.at[i]) for i, (a, b) in enumerate(pairs)]
    for copy in copies:
        copy.start()
    for copy in copies:
        copy.wait()
    x = x_ref[...].astype(jnp.float32).T
    cent = x - jnp.mean(x, 0, keepdims=True)
    rstd = lax.rsqrt(jnp.mean(cent * cent, 0, keepdims=True) + EPS)
    xhat = cent * rstd
    proj = tdot(wm_ref[...], xhat.astype(jnp.bfloat16), 0, 0)
    g = jax.nn.sigmoid(proj[192:256])
    d_gated = tdot(wf_ref[...], rc_ref[...], 1, 1)
    d_attn = d_gated * g
    save_ref[...] = jnp.concatenate([xhat, g, d_gated, jnp.broadcast_to(rstd, (8, 128))], 0)
    for h in range(HEADS):
        lo, hi = h * HEAD_DIM, (h + 1) * HEAD_DIM
        b = bias_ref[h].astype(jnp.float32)
        parts = [proj[lo:hi] * SCALE, d_attn[lo:hi], proj[64 + lo : 64 + hi], proj[128 + lo : 128 + hi]]
        parts += [b[r : r + 1, c * 128 : c * 128 + 128] for r in range(2) for c in range(8)]
        pack_ref[h] = jnp.concatenate(parts, 0).astype(jnp.bfloat16)


GROUPS = [(zl, x) for zl in range(2) for x in range(4)]


def bias_kernel(own_ref, sibling_ref, bias_ref, wide_ref, tmp_ref):
    core = lax.axis_index("core")
    for x in range(4):
        for h in range(8):
            wide_ref[x * 2 + core, h] = own_ref[x, h].astype(jnp.float32)
            wide_ref[x * 2 + 1 - core, h] = sibling_ref[x, h].astype(jnp.float32)
    for i, (zl, x) in enumerate(GROUPS):
        for zh in range(4):
            for half in range(2):
                at = (zh * 2 + half) * 16
                tmp_ref[i, at : at + 16] = wide_ref[x * 2 + half, zl * 4 + zh]
    for i in range(8):
        for c in range(8):
            bias_ref[i * 16 : i * 16 + 16, c * 128 : c * 128 + 128] = tmp_ref[i, pl.ds(c, 16, stride=8)]


def bias_grad_kernel(acc_ref, keep_ref, give_ref, wide_ref, tmp_ref):
    core = lax.axis_index("core")
    for i in range(8):
        for c in range(8):
            tmp_ref[i, pl.ds(c, 16, stride=8)] = acc_ref[i * 16 : i * 16 + 16, c * 128 : c * 128 + 128]
    for i, (zl, x) in enumerate(GROUPS):
        for zh in range(4):
            for half in range(2):
                at = (zh * 2 + half) * 16
                wide_ref[x * 2 + half, zl * 4 + zh] = tmp_ref[i, at : at + 16]
    for x in range(4):
        for h in range(8):
            keep_ref[x, h] = wide_ref[x * 2 + core, h].astype(jnp.bfloat16)
            give_ref[x, h] = wide_ref[x * 2 + 1 - core, h].astype(jnp.bfloat16)


def attend_kernel(pack_ref, kv_in_ref, bias_ref, oq_ref, dkv_ref, acc_ref, kv_ref, t_ref, pair_ref):
    left = lax.broadcasted_iota(jnp.int32, (128, 16), 1) < HEAD_DIM
    blocks = [slice(at, at + 16) for at in range(0, 128, 16)]
    queries, cots, tops, sums, deltas, scaled, attns = [], [], [], [], [], [], []
    for n in range(8):
        dl, lanes = n // 2, slice(n % 2 * 64, n % 2 * 64 + 64)
        kv_ref[n] = jnp.concatenate(
            [kv_in_ref[y, zl * 4 + dl][:, lanes] for zl in range(2) for y in range(8)], 1
        )
        qd = jnp.concatenate([pack_ref[zl * 4 + dl, 0:16][:, lanes] for zl in range(2)], 1)
        rows = qd.astype(jnp.float32).T
        queries.append(jnp.where(left, rows, 0.0))
        cots.append(jnp.where(left, 0.0, rows))
    for n in range(8):
        q = queries[n].astype(jnp.bfloat16)
        top = []
        for i, b in enumerate(blocks):
            if i % 4 == 0:
                scores = tdot(q[i * 16 : i * 16 + 64], kv_ref[n], 1, 0)
            t = scores[i % 4 * 16 : i % 4 * 16 + 16] + bias_ref[b]
            t_ref[n, b] = t
            top.append(jnp.max(t, 1, keepdims=True))
        tops.append(top)
    for n in range(8):
        total = []
        for i, b in enumerate(blocks):
            e = jnp.exp(t_ref[n, b] - tops[n][i])
            total.append(jnp.sum(e, 1, keepdims=True))
            pair_ref[n, 128 + i * 16 : 144 + i * 16] = e.astype(jnp.bfloat16)
        sums.append(jnp.concatenate(total, 0))
    for n in range(8):
        inverse = 1.0 / sums[n]
        attn = tdot(pair_ref[n, 128:256], kv_ref[n], 1, 1) * inverse
        d = (cots[n] * inverse).astype(jnp.bfloat16)
        scaled.append(d)
        attns.append(attn)
        deltas.append(jnp.sum(d.astype(jnp.float32) * attn, 1, keepdims=True))
    for n in range(0, 8, 2):
        for half in (slice(0, 64), slice(64, 128)):
            dps = [tdot(scaled[m][half], kv_ref[m], 1, 0) for m in (n, n + 1)]
            for at in range(0, 64, 16):
                b = slice(half.start + at, half.start + at + 16)
                both = None
                for m, dp in zip((n, n + 1), dps):
                    e = pair_ref[m, 128 + b.start : 128 + b.stop].astype(jnp.float32)
                    ds = e * (dp[at : at + 16] - deltas[m][b])
                    pair_ref[m, b] = ds.astype(jnp.bfloat16)
                    both = ds if both is None else both + ds
                acc_ref[b] = both if n == 0 else acc_ref[b] + both
    outs, grads = [], []
    for n in range(8):
        dq = tdot(pair_ref[n, 0:128], kv_ref[n], 1, 1)
        outs.append(jnp.where(left, dq, attns[n]).T.astype(jnp.bfloat16))
        lhs = jnp.concatenate([queries[n].T, scaled[n].astype(jnp.float32).T], 1)
        grads.append(tdot(lhs.astype(jnp.bfloat16), pair_ref[n], 1, 0).astype(jnp.bfloat16))
    for dl in range(4):
        for zl in range(2):
            part = slice(zl * 64, zl * 64 + 64)
            oq_ref[zl * 4 + dl] = jnp.concatenate([outs[dl * 2 + s][:, part] for s in range(2)], 1)
            for y in range(8):
                r = zl * 8 + y
                part_y = slice(r * 64, r * 64 + 64)
                dkv_ref[y, zl * 4 + dl] = jnp.concatenate(
                    [grads[dl * 2 + s][:, part_y] for s in range(2)], 1
                )


def join_kernel(keep_ref, got_ref, out_ref):
    for x in range(4):
        for h in range(HEADS):
            both = keep_ref[x, h].astype(jnp.float32) + got_ref[x, h].astype(jnp.float32)
            out_ref[x, h] = both.astype(jnp.bfloat16)


def total(blocks):
    acc = blocks[0].astype(jnp.float32)
    for block in blocks[1:]:
        acc += block.astype(jnp.float32)
    return acc.astype(jnp.bfloat16)


def sum_kernel(oq_ref, dkv_ref, db_ref, pack_ref):
    for h in range(HEADS):
        pack_ref[h, 0:16] = oq_ref[h]
        pack_ref[h, 16:32] = total([dkv_ref[y, h] for y in range(8)])
        pack_ref[h, 32:48] = total([db_ref[x, h] for x in range(4)])


def finish_kernel(pack_ref, save_ref, wm_ref, wf_ref, up_ref, dx_ref, db_ref):
    dq, dk, dv, attn = [], [], [], []
    for h in range(HEADS):
        own = pack_ref[h].astype(jnp.float32)
        dq.append(own[0:8] * SCALE)
        attn.append(own[8:16])
        dk.append(own[16:24])
        dv.append(own[24:32])
        for r in range(2):
            db_ref[h, r : r + 1] = jnp.concatenate(
                [own[32 + r * 8 + c : 33 + r * 8 + c] for c in range(8)], 1
            )
    attn = jnp.concatenate(attn, 0)
    xhat, g, d_gated, rstd = save_ref[0:64], save_ref[64:128], save_ref[128:192], save_ref[192:193]
    gated = (g * attn).astype(jnp.bfloat16)
    up_ref[...] = tdot(gated, wf_ref[...], 0, 0).astype(jnp.bfloat16)
    d_gate = d_gated * attn * g * (1.0 - g)
    d_proj = jnp.concatenate(dq + dk + dv + [d_gate], 0).astype(jnp.bfloat16)
    d_normed = tdot(wm_ref[...], d_proj, 1, 0)
    dx = rstd * (
        d_normed
        - jnp.mean(d_normed, 0, keepdims=True)
        - xhat * jnp.mean(d_normed * xhat, 0, keepdims=True)
    )
    dx_ref[...] = dx.T.astype(jnp.bfloat16)


def call(kernel, outs, *args, scratch=(), space=pltpu.VMEM, limit=40):
    return pl.pallas_call(
        kernel,
        out_shape=outs,
        in_specs=[pl.BlockSpec(memory_space=space)] * len(args),
        out_specs=[pl.BlockSpec(memory_space=pltpu.VMEM)] * len(outs),
        scratch_shapes=list(scratch),
        compiler_params=pltpu.CompilerParams(vmem_limit_bytes=limit * 1024 * 1024),
    )(*args)


def shape(*dims, dtype=jnp.bfloat16):
    return jax.ShapeDtypeStruct(dims, dtype)


def exchange(a, axes):
    return lax.all_to_all(a, axes, 0, 0, tiled=True)


def swap_core(a):
    return lax.ppermute(a, "core", [(0, 1), (1, 0)])


def per_device(x, bias, wm, wf, rc):
    f32 = jnp.float32
    pack, saved = call(
        project_kernel,
        [shape(8, 48, 128), shape(200, 128, dtype=f32)],
        x.reshape(128, 64), rc.reshape(128, 64), wm, wf, bias,
        scratch=[pltpu.VMEM((128, 64), jnp.bfloat16), pltpu.VMEM((128, 64), jnp.bfloat16),
                 pltpu.VMEM((64, 256), jnp.bfloat16), pltpu.VMEM((64, 64), jnp.bfloat16),
                 pltpu.VMEM((8, 2, 1024), jnp.bfloat16), pltpu.SemaphoreType.DMA((5,))],
        space=pltpu.HBM, limit=60,
    )
    pack = exchange(pack, HEAD_AXES)
    rows = pack[:, 32:48]
    rows = exchange(jnp.broadcast_to(rows[None], (4,) + rows.shape), ("x",))
    own, rows = lax.optimization_barrier((pack[:, 16:32], rows))
    kv = exchange(jnp.broadcast_to(own[None], (8,) + own.shape), KEY_AXES)
    layout = [pltpu.VMEM((8, 8, 16, 128), f32), pltpu.VMEM((8, 128, 128), f32)]
    (bias_rows,) = call(bias_kernel, [shape(128, 1024, dtype=f32)], rows, swap_core(rows), scratch=layout)
    block, quad, octet = shape(8, 16, 128), shape(4, 8, 16, 128), shape(8, 8, 16, 128)
    oq, dkv, acc = call(
        attend_kernel,
        [block, octet, shape(128, 1024, dtype=f32)],
        pack, kv, bias_rows,
        scratch=[pltpu.VMEM((8, 16, 1024), jnp.bfloat16), pltpu.VMEM((8, 128, 1024), f32),
                 pltpu.VMEM((8, 256, 1024), jnp.bfloat16)],
    )
    dkv = exchange(dkv, KEY_AXES)
    keep, give = call(bias_grad_kernel, [quad, quad], acc, scratch=layout)
    (db,) = call(join_kernel, [quad], keep, swap_core(give))
    dkv, db = lax.optimization_barrier((dkv, db))
    db = exchange(db, ("x",))
    (back,) = call(sum_kernel, [shape(8, 48, 128)], oq, dkv, db)
    back = exchange(back, HEAD_AXES)
    update, dx, d_bias = call(
        finish_kernel,
        [shape(128, 64), shape(128, 64), shape(8, 2, 1024, dtype=f32)],
        back, saved, wm, wf,
    )
    return update.reshape(2, 64, 64), dx.reshape(2, 64, 64), d_bias


def solution(mesh):
    fine = Mesh(mesh.devices.reshape(4, 4, 2, 2, 8), DEPTH + RES)
    tokens = P(DEPTH, RES, None)
    rows = P(None, RES + DEPTH, None)
    return jax.shard_map(
        per_device,
        mesh=fine,
        in_specs=(tokens, rows, P(), P(), tokens),
        out_specs=(tokens, tokens, rows),
        check_vma=False,
    )
```

```python
import math

import jax
import jax.numpy as jnp
from jax import lax
from jax.experimental import pallas as pl
from jax.experimental.pallas import tpu as pltpu
from jax.sharding import Mesh, PartitionSpec as P

HEADS = 8
HEAD_DIM = 8
EPS = 1e-05
SCALE = 1.0 / math.sqrt(HEAD_DIM)

DEPTH = ("x", "zh", "core")
RES = ("zl", "y")
HEAD_AXES = ("zl", "zh")
KEY_AXES = ("y",)


def tdot(a, b, ca, cb):
    return lax.dot_general(a, b, (((ca,), (cb,)), ((), ())), preferred_element_type=jnp.float32)


def project_kernel(x_hbm, rc_hbm, wm_hbm, wf_hbm, bias_hbm, pack_ref, save_ref,
                   x_ref, rc_ref, wm_ref, wf_ref, bias_ref, sems):
    pairs = [(x_hbm, x_ref), (wm_hbm, wm_ref), (rc_hbm, rc_ref), (wf_hbm, wf_ref), (bias_hbm, bias_ref)]
    copies = [pltpu.make_async_copy(a, b, sems.at[i]) for i, (a, b) in enumerate(pairs)]
    for copy in copies:
        copy.start()
    copies[0].wait()
    x = x_ref[...].astype(jnp.float32).T
    cent = x - jnp.mean(x, 0, keepdims=True)
    rstd = lax.rsqrt(jnp.mean(cent * cent, 0, keepdims=True) + EPS)
    xhat = cent * rstd
    copies[1].wait()
    proj = tdot(wm_ref[...], xhat.astype(jnp.bfloat16), 0, 0)
    g = jax.nn.sigmoid(proj[192:256])
    copies[2].wait()
    copies[3].wait()
    copies[4].wait()
    d_gated = tdot(wf_ref[...], rc_ref[...], 1, 1)
    d_attn = d_gated * g
    save_ref[...] = jnp.concatenate([xhat, g, d_gated, jnp.broadcast_to(rstd, (8, 128))], 0)
    for h in range(HEADS):
        lo, hi = h * HEAD_DIM, (h + 1) * HEAD_DIM
        b = bias_ref[h].astype(jnp.float32)
        parts = [proj[lo:hi] * SCALE, d_attn[lo:hi], proj[64 + lo : 64 + hi], proj[128 + lo : 128 + hi]]
        parts += [b[r : r + 1, c * 128 : c * 128 + 128] for r in range(2) for c in range(8)]
        pack_ref[h] = jnp.concatenate(parts, 0).astype(jnp.bfloat16)


GROUPS = [(zl, x) for zl in range(2) for x in range(4)]


def bias_kernel(own_ref, sibling_ref, bias_ref, wide_ref, tmp_ref):
    core = lax.axis_index("core")
    for x in range(4):
        for h in range(8):
            wide_ref[x * 2 + core, h] = own_ref[x, h].astype(jnp.float32)
            wide_ref[x * 2 + 1 - core, h] = sibling_ref[x, h].astype(jnp.float32)
    for i, (zl, x) in enumerate(GROUPS):
        for zh in range(4):
            for half in range(2):
                at = (zh * 2 + half) * 16
                tmp_ref[i, at : at + 16] = wide_ref[x * 2 + half, zl * 4 + zh]
    for i in range(8):
        for c in range(8):
            bias_ref[i * 16 : i * 16 + 16, c * 128 : c * 128 + 128] = tmp_ref[i, pl.ds(c, 16, stride=8)]


def bias_grad_kernel(acc_ref, keep_ref, give_ref, wide_ref, tmp_ref):
    core = lax.axis_index("core")
    for i in range(8):
        for c in range(8):
            tmp_ref[i, pl.ds(c, 16, stride=8)] = acc_ref[i * 16 : i * 16 + 16, c * 128 : c * 128 + 128]
    for i, (zl, x) in enumerate(GROUPS):
        for zh in range(4):
            for half in range(2):
                at = (zh * 2 + half) * 16
                wide_ref[x * 2 + half, zl * 4 + zh] = tmp_ref[i, at : at + 16]
    for x in range(4):
        for h in range(8):
            keep_ref[x, h] = wide_ref[x * 2 + core, h].astype(jnp.bfloat16)
            give_ref[x, h] = wide_ref[x * 2 + 1 - core, h].astype(jnp.bfloat16)


def attend_kernel(pack_ref, kv_in_ref, bias_ref, oq_ref, dkv_ref, acc_ref, kv_ref, t_ref, pair_ref):
    left = lax.broadcasted_iota(jnp.int32, (128, 16), 1) < HEAD_DIM
    blocks = [slice(at, at + 16) for at in range(0, 128, 16)]
    upper = lax.broadcasted_iota(jnp.int32, (16, 128), 0) < HEAD_DIM
    state = [{} for n in range(8)]

    def score(n, at):
        dl, lanes = n // 2, slice(n % 2 * 64, n % 2 * 64 + 64)
        kv_ref[n] = jnp.concatenate(
            [kv_in_ref[y, zl * 4 + dl][:, lanes] for zl in range(2) for y in range(8)], 1
        )
        qd = jnp.concatenate([pack_ref[zl * 4 + dl, 0:16][:, lanes] for zl in range(2)], 1)
        qd = qd.astype(jnp.float32)
        rows = qd.T
        q = jnp.where(left, rows, 0.0).astype(jnp.bfloat16)
        at["q"], at["d"] = jnp.where(upper, qd, 0.0), jnp.where(left, 0.0, rows)
        scores = tdot(q, kv_ref[n], 1, 0)
        at["top"] = []
        for b in blocks:
            t = scores[b] + bias_ref[b]
            t_ref[n, b] = t
            at["top"].append(jnp.max(t, 1, keepdims=True))

    def exponentiate(n, at):
        total = []
        for i, b in enumerate(blocks):
            e = jnp.exp(t_ref[n, b] - at["top"][i])
            total.append(jnp.sum(e, 1, keepdims=True))
            pair_ref[n, 128 + i * 16 : 144 + i * 16] = e.astype(jnp.bfloat16)
        at["sum"] = jnp.concatenate(total, 0)

    def attend(n, at):
        inverse = 1.0 / at["sum"]
        at["attn"] = tdot(pair_ref[n, 128:256], kv_ref[n], 1, 1) * inverse
        at["scaled"] = (at["d"] * inverse).astype(jnp.bfloat16)
        at["delta"] = jnp.sum(at["scaled"].astype(jnp.float32) * at["attn"], 1, keepdims=True)

    def differentiate(n, at):
        dp = tdot(at["scaled"], kv_ref[n], 1, 0)
        for i, b in enumerate(blocks):
            e = pair_ref[n, 128 + i * 16 : 144 + i * 16].astype(jnp.float32)
            ds = e * (dp[b] - at["delta"][b])
            pair_ref[n, b] = ds.astype(jnp.bfloat16)
            acc_ref[b] = ds if n == 0 else acc_ref[b] + ds

    def multiply(n, at):
        dq = tdot(pair_ref[n, 0:128], kv_ref[n], 1, 1)
        at["out"] = jnp.where(left, dq, at["attn"]).T.astype(jnp.bfloat16)
        lhs = jnp.concatenate([at["q"], at["scaled"].astype(jnp.float32).T], 1)
        at["grad"] = tdot(lhs.astype(jnp.bfloat16), pair_ref[n], 1, 0).astype(jnp.bfloat16)

    stages = [score, exponentiate, attend, differentiate, multiply]
    for step in range(8 + len(stages) - 1):
        for lag, stage in enumerate(stages):
            if 0 <= step - lag < 8:
                stage(step - lag, state[step - lag])
    outs, grads = [at["out"] for at in state], [at["grad"] for at in state]
    for dl in range(4):
        for zl in range(2):
            part = slice(zl * 64, zl * 64 + 64)
            oq_ref[zl * 4 + dl] = jnp.concatenate([outs[dl * 2 + s][:, part] for s in range(2)], 1)
            for y in range(8):
                r = zl * 8 + y
                part_y = slice(r * 64, r * 64 + 64)
                dkv_ref[y, zl * 4 + dl] = jnp.concatenate(
                    [grads[dl * 2 + s][:, part_y] for s in range(2)], 1
                )


def join_kernel(keep_ref, got_ref, out_ref):
    for x in range(4):
        for h in range(HEADS):
            both = keep_ref[x, h].astype(jnp.float32) + got_ref[x, h].astype(jnp.float32)
            out_ref[x, h] = both.astype(jnp.bfloat16)


def total(blocks):
    acc = blocks[0].astype(jnp.float32)
    for block in blocks[1:]:
        acc += block.astype(jnp.float32)
    return acc.astype(jnp.bfloat16)


def sum_kernel(oq_ref, dkv_ref, db_ref, pack_ref):
    for h in range(HEADS):
        pack_ref[h, 0:16] = oq_ref[h]
        pack_ref[h, 16:32] = total([dkv_ref[y, h] for y in range(8)])
        pack_ref[h, 32:48] = total([db_ref[x, h] for x in range(4)])


def finish_kernel(pack_ref, save_ref, wm_ref, wf_ref, up_ref, dx_ref, db_ref):
    dq, dk, dv, attn = [], [], [], []
    for h in range(HEADS):
        own = pack_ref[h].astype(jnp.float32)
        dq.append(own[0:8] * SCALE)
        attn.append(own[8:16])
        dk.append(own[16:24])
        dv.append(own[24:32])
        for r in range(2):
            db_ref[h, r : r + 1] = jnp.concatenate(
                [own[32 + r * 8 + c : 33 + r * 8 + c] for c in range(8)], 1
            )
    attn = jnp.concatenate(attn, 0)
    xhat, g, d_gated, rstd = save_ref[0:64], save_ref[64:128], save_ref[128:192], save_ref[192:193]
    gated = (g * attn).astype(jnp.bfloat16)
    up_ref[...] = tdot(gated, wf_ref[...], 0, 0).astype(jnp.bfloat16)
    d_gate = d_gated * attn * g * (1.0 - g)
    d_proj = jnp.concatenate(dq + dk + dv + [d_gate], 0).astype(jnp.bfloat16)
    d_normed = tdot(wm_ref[...], d_proj, 1, 0)
    dx = rstd * (
        d_normed
        - jnp.mean(d_normed, 0, keepdims=True)
        - xhat * jnp.mean(d_normed * xhat, 0, keepdims=True)
    )
    dx_ref[...] = dx.T.astype(jnp.bfloat16)


def call(kernel, outs, *args, scratch=(), space=pltpu.VMEM, limit=40):
    return pl.pallas_call(
        kernel,
        out_shape=outs,
        in_specs=[pl.BlockSpec(memory_space=space)] * len(args),
        out_specs=[pl.BlockSpec(memory_space=pltpu.VMEM)] * len(outs),
        scratch_shapes=list(scratch),
        compiler_params=pltpu.CompilerParams(vmem_limit_bytes=limit * 1024 * 1024),
    )(*args)


def shape(*dims, dtype=jnp.bfloat16):
    return jax.ShapeDtypeStruct(dims, dtype)


def exchange(a, axes):
    return lax.all_to_all(a, axes, 0, 0, tiled=True)


def swap_core(a):
    return lax.ppermute(a, "core", [(0, 1), (1, 0)])


def per_device(x, bias, wm, wf, rc):
    f32 = jnp.float32
    pack, saved = call(
        project_kernel,
        [shape(8, 48, 128), shape(200, 128, dtype=f32)],
        x.reshape(128, 64), rc.reshape(128, 64), wm, wf, bias,
        scratch=[pltpu.VMEM((128, 64), jnp.bfloat16), pltpu.VMEM((128, 64), jnp.bfloat16),
                 pltpu.VMEM((64, 256), jnp.bfloat16), pltpu.VMEM((64, 64), jnp.bfloat16),
                 pltpu.VMEM((8, 2, 1024), jnp.bfloat16), pltpu.SemaphoreType.DMA((5,))],
        space=pltpu.HBM, limit=60,
    )
    pack = exchange(pack, HEAD_AXES)
    rows = pack[:, 32:48]
    rows = exchange(jnp.broadcast_to(rows[None], (4,) + rows.shape), ("x",))
    own, rows = lax.optimization_barrier((pack[:, 16:32], rows))
    kv = exchange(jnp.broadcast_to(own[None], (8,) + own.shape), KEY_AXES)
    layout = [pltpu.VMEM((8, 8, 16, 128), f32), pltpu.VMEM((8, 128, 128), f32)]
    (bias_rows,) = call(bias_kernel, [shape(128, 1024, dtype=f32)], rows, swap_core(rows), scratch=layout)
    block, quad, octet = shape(8, 16, 128), shape(4, 8, 16, 128), shape(8, 8, 16, 128)
    oq, dkv, acc = call(
        attend_kernel,
        [block, octet, shape(128, 1024, dtype=f32)],
        pack, kv, bias_rows,
        scratch=[pltpu.VMEM((8, 16, 1024), jnp.bfloat16), pltpu.VMEM((8, 128, 1024), f32),
                 pltpu.VMEM((8, 256, 1024), jnp.bfloat16)],
    )
    dkv = exchange(dkv, KEY_AXES)
    keep, give = call(bias_grad_kernel, [quad, quad], acc, scratch=layout)
    (db,) = call(join_kernel, [quad], keep, swap_core(give))
    dkv, db = lax.optimization_barrier((dkv, db))
    db = exchange(db, ("x",))
    (back,) = call(sum_kernel, [shape(8, 48, 128)], oq, dkv, db)
    back = exchange(back, HEAD_AXES)
    update, dx, d_bias = call(
        finish_kernel,
        [shape(128, 64), shape(128, 64), shape(8, 2, 1024, dtype=f32)],
        back, saved, wm, wf,
    )
    return update.reshape(2, 64, 64), dx.reshape(2, 64, 64), d_bias


def solution(mesh):
    fine = Mesh(mesh.devices.reshape(4, 4, 2, 2, 8), DEPTH + RES)
    tokens = P(DEPTH, RES, None)
    rows = P(None, RES + DEPTH, None)
    return jax.shard_map(
        per_device,
        mesh=fine,
        in_specs=(tokens, rows, P(), P(), tokens),
        out_specs=(tokens, tokens, rows),
        check_vma=False,
    )
```

```python
import math

import jax
import jax.numpy as jnp
from jax import lax
from jax.experimental import pallas as pl
from jax.experimental.pallas import tpu as pltpu
from jax.sharding import Mesh, PartitionSpec as P

HEADS = 8
HEAD_DIM = 8
EPS = 1e-05
SCALE = 1.0 / math.sqrt(HEAD_DIM)

DEPTH = ("x", "zh", "core")
RES = ("zl", "y")
HEAD_AXES = ("zl", "zh")
KEY_AXES = ("y",)


def tdot(a, b, ca, cb):
    return lax.dot_general(a, b, (((ca,), (cb,)), ((), ())), preferred_element_type=jnp.float32)


def project_kernel(x_hbm, rc_hbm, wm_hbm, wf_hbm, bias_hbm, pack_ref, save_ref,
                   x_ref, rc_ref, wm_ref, wf_ref, bias_ref, sems):
    pairs = [(x_hbm, x_ref), (wm_hbm, wm_ref), (rc_hbm, rc_ref), (wf_hbm, wf_ref), (bias_hbm, bias_ref)]
    copies = [pltpu.make_async_copy(a, b, sems.at[i]) for i, (a, b) in enumerate(pairs)]
    for copy in copies:
        copy.start()
    for copy in copies:
        copy.wait()
    x = x_ref[...].astype(jnp.float32).T
    cent = x - jnp.mean(x, 0, keepdims=True)
    rstd = lax.rsqrt(jnp.mean(cent * cent, 0, keepdims=True) + EPS)
    xhat = cent * rstd
    proj = tdot(wm_ref[...], xhat.astype(jnp.bfloat16), 0, 0)
    g = jax.nn.sigmoid(proj[192:256])
    d_gated = tdot(wf_ref[...], rc_ref[...], 1, 1)
    d_attn = d_gated * g
    save_ref[...] = jnp.concatenate([xhat, g, d_gated, jnp.broadcast_to(rstd, (8, 128))], 0)
    for h in range(HEADS):
        lo, hi = h * HEAD_DIM, (h + 1) * HEAD_DIM
        b = bias_ref[h].astype(jnp.float32)
        parts = [proj[lo:hi] * SCALE, d_attn[lo:hi], proj[64 + lo : 64 + hi], proj[128 + lo : 128 + hi]]
        parts += [b[r : r + 1, c * 128 : c * 128 + 128] for r in range(2) for c in range(8)]
        pack_ref[h] = jnp.concatenate(parts, 0).astype(jnp.bfloat16)


GROUPS = [(zl, x) for zl in range(2) for x in range(4)]


def bias_kernel(own_ref, sibling_ref, bias_ref, wide_ref, tmp_ref):
    core = lax.axis_index("core")
    for x in range(4):
        for h in range(8):
            wide_ref[x * 2 + core, h] = own_ref[x, h].astype(jnp.float32)
            wide_ref[x * 2 + 1 - core, h] = sibling_ref[x, h].astype(jnp.float32)
    for i, (zl, x) in enumerate(GROUPS):
        for zh in range(4):
            for half in range(2):
                at = (zh * 2 + half) * 16
                tmp_ref[i, at : at + 16] = wide_ref[x * 2 + half, zl * 4 + zh]
    for i in range(8):
        for c in range(8):
            bias_ref[i * 16 : i * 16 + 16, c * 128 : c * 128 + 128] = tmp_ref[i, pl.ds(c, 16, stride=8)]


def bias_grad_kernel(acc_ref, keep_ref, give_ref, wide_ref, tmp_ref):
    core = lax.axis_index("core")
    for i in range(8):
        for c in range(8):
            tmp_ref[i, pl.ds(c, 16, stride=8)] = acc_ref[i * 16 : i * 16 + 16, c * 128 : c * 128 + 128]
    for i, (zl, x) in enumerate(GROUPS):
        for zh in range(4):
            for half in range(2):
                at = (zh * 2 + half) * 16
                wide_ref[x * 2 + half, zl * 4 + zh] = tmp_ref[i, at : at + 16]
    for x in range(4):
        for h in range(8):
            keep_ref[x, h] = wide_ref[x * 2 + core, h].astype(jnp.bfloat16)
            give_ref[x, h] = wide_ref[x * 2 + 1 - core, h].astype(jnp.bfloat16)


def attend_kernel(pack_ref, kv_in_ref, bias_ref, oq_ref, dkv_ref, acc_ref, kv_ref, t_ref, pair_ref):
    left = lax.broadcasted_iota(jnp.int32, (128, 16), 1) < HEAD_DIM
    blocks = [slice(at, at + 16) for at in range(0, 128, 16)]
    upper = lax.broadcasted_iota(jnp.int32, (16, 128), 0) < HEAD_DIM
    state = [{} for n in range(8)]
    ones = jnp.ones((16, 1024), jnp.bfloat16)

    def score(n, at):
        dl, lanes = n // 2, slice(n % 2 * 64, n % 2 * 64 + 64)
        kv_ref[n, 0:16] = jnp.concatenate(
            [kv_in_ref[y, zl * 4 + dl][:, lanes] for zl in range(2) for y in range(8)], 1
        )
        kv_ref[n, 16:32] = ones
        qd = jnp.concatenate([pack_ref[zl * 4 + dl, 0:16][:, lanes] for zl in range(2)], 1)
        qd = qd.astype(jnp.float32)
        rows = qd.T
        q = jnp.where(left, rows, 0.0).astype(jnp.bfloat16)
        at["q"], at["d"] = jnp.where(upper, qd, 0.0), jnp.where(left, 0.0, rows)
        scores = tdot(q, kv_ref[n, 0:16], 1, 0)
        at["top"] = []
        for b in blocks:
            t = scores[b] + bias_ref[b]
            t_ref[n, b] = t
            at["top"].append(jnp.max(t, 1, keepdims=True))

    def exponentiate(n, at):
        for i, b in enumerate(blocks):
            e = jnp.exp(t_ref[n, b] - at["top"][i])
            pair_ref[n, 128 + i * 16 : 144 + i * 16] = e.astype(jnp.bfloat16)

    def attend(n, at):
        summed = tdot(pair_ref[n, 128:256], kv_ref[n], 1, 1)
        inverse = 1.0 / summed[:, 16:32]
        at["attn"] = summed[:, 0:16] * inverse
        at["scaled"] = (at["d"] * inverse).astype(jnp.bfloat16)
        at["delta"] = jnp.sum(at["scaled"].astype(jnp.float32) * at["attn"], 1, keepdims=True)

    def differentiate(n, at):
        dp = tdot(at["scaled"], kv_ref[n, 0:16], 1, 0)
        for i, b in enumerate(blocks):
            e = pair_ref[n, 128 + i * 16 : 144 + i * 16].astype(jnp.float32)
            ds = e * (dp[b] - at["delta"][b])
            pair_ref[n, b] = ds.astype(jnp.bfloat16)
            acc_ref[b] = ds if n == 0 else acc_ref[b] + ds

    def multiply(n, at):
        dq = tdot(pair_ref[n, 0:128], kv_ref[n, 0:16], 1, 1)
        at["out"] = jnp.where(left, dq, at["attn"]).T.astype(jnp.bfloat16)
        lhs = jnp.concatenate([at["q"], at["scaled"].astype(jnp.float32).T], 1)
        at["grad"] = tdot(lhs.astype(jnp.bfloat16), pair_ref[n], 1, 0).astype(jnp.bfloat16)

    stages = [score, exponentiate, attend, differentiate, multiply]
    for step in range(8 + len(stages) - 1):
        for lag, stage in enumerate(stages):
            if 0 <= step - lag < 8:
                stage(step - lag, state[step - lag])
    outs, grads = [at["out"] for at in state], [at["grad"] for at in state]
    for dl in range(4):
        for zl in range(2):
            part = slice(zl * 64, zl * 64 + 64)
            oq_ref[zl * 4 + dl] = jnp.concatenate([outs[dl * 2 + s][:, part] for s in range(2)], 1)
            for y in range(8):
                r = zl * 8 + y
                part_y = slice(r * 64, r * 64 + 64)
                dkv_ref[y, zl * 4 + dl] = jnp.concatenate(
                    [grads[dl * 2 + s][:, part_y] for s in range(2)], 1
                )


def join_kernel(keep_ref, got_ref, out_ref):
    for x in range(4):
        for h in range(HEADS):
            both = keep_ref[x, h].astype(jnp.float32) + got_ref[x, h].astype(jnp.float32)
            out_ref[x, h] = both.astype(jnp.bfloat16)


def total(blocks):
    acc = blocks[0].astype(jnp.float32)
    for block in blocks[1:]:
        acc += block.astype(jnp.float32)
    return acc.astype(jnp.bfloat16)


def sum_kernel(oq_ref, dkv_ref, db_ref, pack_ref):
    for h in range(HEADS):
        pack_ref[h, 0:16] = oq_ref[h]
        pack_ref[h, 16:32] = total([dkv_ref[y, h] for y in range(8)])
        pack_ref[h, 32:48] = total([db_ref[x, h] for x in range(4)])


def finish_kernel(pack_ref, save_ref, wm_ref, wf_ref, up_ref, dx_ref, db_ref):
    dq, dk, dv, attn = [], [], [], []
    for h in range(HEADS):
        own = pack_ref[h].astype(jnp.float32)
        dq.append(own[0:8] * SCALE)
        attn.append(own[8:16])
        dk.append(own[16:24])
        dv.append(own[24:32])
        for r in range(2):
            db_ref[h, r : r + 1] = jnp.concatenate(
                [own[32 + r * 8 + c : 33 + r * 8 + c] for c in range(8)], 1
            )
    attn = jnp.concatenate(attn, 0)
    xhat, g, d_gated, rstd = save_ref[0:64], save_ref[64:128], save_ref[128:192], save_ref[192:193]
    gated = (g * attn).astype(jnp.bfloat16)
    up_ref[...] = tdot(gated, wf_ref[...], 0, 0).astype(jnp.bfloat16)
    d_gate = d_gated * attn * g * (1.0 - g)
    d_proj = jnp.concatenate(dq + dk + dv + [d_gate], 0).astype(jnp.bfloat16)
    d_normed = tdot(wm_ref[...], d_proj, 1, 0)
    dx = rstd * (
        d_normed
        - jnp.mean(d_normed, 0, keepdims=True)
        - xhat * jnp.mean(d_normed * xhat, 0, keepdims=True)
    )
    dx_ref[...] = dx.T.astype(jnp.bfloat16)


def call(kernel, outs, *args, scratch=(), space=pltpu.VMEM, limit=40):
    return pl.pallas_call(
        kernel,
        out_shape=outs,
        in_specs=[pl.BlockSpec(memory_space=space)] * len(args),
        out_specs=[pl.BlockSpec(memory_space=pltpu.VMEM)] * len(outs),
        scratch_shapes=list(scratch),
        compiler_params=pltpu.CompilerParams(vmem_limit_bytes=limit * 1024 * 1024),
    )(*args)


def shape(*dims, dtype=jnp.bfloat16):
    return jax.ShapeDtypeStruct(dims, dtype)


def exchange(a, axes):
    return lax.all_to_all(a, axes, 0, 0, tiled=True)


def swap_core(a):
    return lax.ppermute(a, "core", [(0, 1), (1, 0)])


def per_device(x, bias, wm, wf, rc):
    f32 = jnp.float32
    pack, saved = call(
        project_kernel,
        [shape(8, 48, 128), shape(200, 128, dtype=f32)],
        x.reshape(128, 64), rc.reshape(128, 64), wm, wf, bias,
        scratch=[pltpu.VMEM((128, 64), jnp.bfloat16), pltpu.VMEM((128, 64), jnp.bfloat16),
                 pltpu.VMEM((64, 256), jnp.bfloat16), pltpu.VMEM((64, 64), jnp.bfloat16),
                 pltpu.VMEM((8, 2, 1024), jnp.bfloat16), pltpu.SemaphoreType.DMA((5,))],
        space=pltpu.HBM, limit=60,
    )
    pack = exchange(pack, HEAD_AXES)
    rows = pack[:, 32:48]
    rows = exchange(jnp.broadcast_to(rows[None], (4,) + rows.shape), ("x",))
    own = jnp.broadcast_to(pack[None, :, 16:32], (8, 8, 16, 128))
    own, rows = lax.optimization_barrier((own, rows))
    kv = exchange(own, KEY_AXES)
    layout = [pltpu.VMEM((8, 8, 16, 128), f32), pltpu.VMEM((8, 128, 128), f32)]
    (bias_rows,) = call(bias_kernel, [shape(128, 1024, dtype=f32)], rows, swap_core(rows), scratch=layout)
    block, quad, octet = shape(8, 16, 128), shape(4, 8, 16, 128), shape(8, 8, 16, 128)
    oq, dkv, acc = call(
        attend_kernel,
        [block, octet, shape(128, 1024, dtype=f32)],
        pack, kv, bias_rows,
        scratch=[pltpu.VMEM((8, 32, 1024), jnp.bfloat16), pltpu.VMEM((8, 128, 1024), f32),
                 pltpu.VMEM((8, 256, 1024), jnp.bfloat16)],
    )
    dkv = exchange(dkv, KEY_AXES)
    keep, give = call(bias_grad_kernel, [quad, quad], acc, scratch=layout)
    (db,) = call(join_kernel, [quad], keep, swap_core(give))
    dkv, db = lax.optimization_barrier((dkv, db))
    db = exchange(db, ("x",))
    (back,) = call(sum_kernel, [shape(8, 48, 128)], oq, dkv, db)
    back = exchange(back, HEAD_AXES)
    update, dx, d_bias = call(
        finish_kernel,
        [shape(128, 64), shape(128, 64), shape(8, 2, 1024, dtype=f32)],
        back, saved, wm, wf,
    )
    return update.reshape(2, 64, 64), dx.reshape(2, 64, 64), d_bias


def solution(mesh):
    fine = Mesh(mesh.devices.reshape(4, 4, 2, 2, 8), DEPTH + RES)
    tokens = P(DEPTH, RES, None)
    rows = P(None, RES + DEPTH, None)
    return jax.shard_map(
        per_device,
        mesh=fine,
        in_specs=(tokens, rows, P(), P(), tokens),
        out_specs=(tokens, tokens, rows),
        check_vma=False,
    )
```

```python
import math

import jax
import jax.numpy as jnp
from jax import lax
from jax.experimental import pallas as pl
from jax.experimental.pallas import tpu as pltpu
from jax.sharding import Mesh, PartitionSpec as P

HEADS = 8
PEER = [y % 4 * 2 + y // 4 for y in range(8)]
HEAD_DIM = 8
EPS = 1e-05
SCALE = 1.0 / math.sqrt(HEAD_DIM)

DEPTH = ("x", "zh", "core")
RES = ("zl", "yh", "yl")
HEAD_AXES = ("zl", "zh")
KEY_AXES = ("yl", "yh")


def tdot(a, b, ca, cb):
    return lax.dot_general(a, b, (((ca,), (cb,)), ((), ())), preferred_element_type=jnp.float32)


def project_kernel(x_hbm, rc_hbm, wm_hbm, wf_hbm, bias_hbm, pack_ref, save_ref,
                   x_ref, rc_ref, wm_ref, wf_ref, bias_ref, sems):
    pairs = [(x_hbm, x_ref), (wm_hbm, wm_ref), (rc_hbm, rc_ref), (wf_hbm, wf_ref), (bias_hbm, bias_ref)]
    copies = [pltpu.make_async_copy(a, b, sems.at[i]) for i, (a, b) in enumerate(pairs)]
    for copy in copies:
        copy.start()
    for copy in copies:
        copy.wait()
    x = x_ref[...].astype(jnp.float32).T
    cent = x - jnp.mean(x, 0, keepdims=True)
    rstd = lax.rsqrt(jnp.mean(cent * cent, 0, keepdims=True) + EPS)
    xhat = cent * rstd
    proj = tdot(wm_ref[...], xhat.astype(jnp.bfloat16), 0, 0)
    g = jax.nn.sigmoid(proj[192:256])
    d_gated = tdot(wf_ref[...], rc_ref[...], 1, 1)
    d_attn = d_gated * g
    save_ref[...] = jnp.concatenate([xhat, g, d_gated, jnp.broadcast_to(rstd, (8, 128))], 0)
    for h in range(HEADS):
        lo, hi = h * HEAD_DIM, (h + 1) * HEAD_DIM
        b = bias_ref[h].astype(jnp.float32)
        parts = [proj[lo:hi] * SCALE, d_attn[lo:hi], proj[64 + lo : 64 + hi], proj[128 + lo : 128 + hi]]
        parts += [b[r : r + 1, c * 128 : c * 128 + 128] for r in range(2) for c in range(8)]
        pack_ref[h] = jnp.concatenate(parts, 0).astype(jnp.bfloat16)


GROUPS = [(zl, x) for zl in range(2) for x in range(4)]


def bias_kernel(own_ref, sibling_ref, bias_ref, wide_ref, tmp_ref):
    core = lax.axis_index("core")
    for x in range(4):
        for h in range(8):
            wide_ref[x * 2 + core, h] = own_ref[x, h].astype(jnp.float32)
            wide_ref[x * 2 + 1 - core, h] = sibling_ref[x, h].astype(jnp.float32)
    for i, (zl, x) in enumerate(GROUPS):
        for zh in range(4):
            for half in range(2):
                at = (zh * 2 + half) * 16
                tmp_ref[i, at : at + 16] = wide_ref[x * 2 + half, zl * 4 + zh]
    for i in range(8):
        for c in range(8):
            bias_ref[i * 16 : i * 16 + 16, c * 128 : c * 128 + 128] = tmp_ref[i, pl.ds(c, 16, stride=8)]


def bias_grad_kernel(acc_ref, keep_ref, give_ref, wide_ref, tmp_ref):
    core = lax.axis_index("core")
    for i in range(8):
        for c in range(8):
            tmp_ref[i, pl.ds(c, 16, stride=8)] = acc_ref[i * 16 : i * 16 + 16, c * 128 : c * 128 + 128]
    for i, (zl, x) in enumerate(GROUPS):
        for zh in range(4):
            for half in range(2):
                at = (zh * 2 + half) * 16
                wide_ref[x * 2 + half, zl * 4 + zh] = tmp_ref[i, at : at + 16]
    for x in range(4):
        for h in range(8):
            keep_ref[x, h] = wide_ref[x * 2 + core, h].astype(jnp.bfloat16)
            give_ref[x, h] = wide_ref[x * 2 + 1 - core, h].astype(jnp.bfloat16)


def attend_kernel(pack_ref, kv_in_ref, bias_ref, oq_ref, dkv_ref, acc_ref, kv_ref, t_ref, pair_ref):
    left = lax.broadcasted_iota(jnp.int32, (128, 16), 1) < HEAD_DIM
    blocks = [slice(at, at + 16) for at in range(0, 128, 16)]
    upper = lax.broadcasted_iota(jnp.int32, (16, 128), 0) < HEAD_DIM
    state = [{} for n in range(8)]
    ones = jnp.ones((16, 1024), jnp.bfloat16)

    def score(n, at):
        dl, lanes = n // 2, slice(n % 2 * 64, n % 2 * 64 + 64)
        kv_ref[n, 0:16] = jnp.concatenate(
            [kv_in_ref[PEER[y], zl * 4 + dl][:, lanes] for zl in range(2) for y in range(8)], 1
        )
        kv_ref[n, 16:32] = ones
        qd = jnp.concatenate([pack_ref[zl * 4 + dl, 0:16][:, lanes] for zl in range(2)], 1)
        qd = qd.astype(jnp.float32)
        rows = qd.T
        q = jnp.where(left, rows, 0.0).astype(jnp.bfloat16)
        at["q"], at["d"] = jnp.where(upper, qd, 0.0), jnp.where(left, 0.0, rows)
        scores = tdot(q, kv_ref[n, 0:16], 1, 0)
        at["top"] = []
        for b in blocks:
            t = scores[b] + bias_ref[b]
            t_ref[n, b] = t
            at["top"].append(jnp.max(t, 1, keepdims=True))

    def exponentiate(n, at):
        for i, b in enumerate(blocks):
            e = jnp.exp(t_ref[n, b] - at["top"][i])
            pair_ref[n, 128 + i * 16 : 144 + i * 16] = e.astype(jnp.bfloat16)

    def attend(n, at):
        summed = tdot(pair_ref[n, 128:256], kv_ref[n], 1, 1)
        inverse = 1.0 / summed[:, 16:32]
        at["attn"] = summed[:, 0:16] * inverse
        at["scaled"] = (at["d"] * inverse).astype(jnp.bfloat16)
        at["delta"] = jnp.sum(at["scaled"].astype(jnp.float32) * at["attn"], 1, keepdims=True)

    def differentiate(n, at):
        dp = tdot(at["scaled"], kv_ref[n, 0:16], 1, 0)
        for i, b in enumerate(blocks):
            e = pair_ref[n, 128 + i * 16 : 144 + i * 16].astype(jnp.float32)
            ds = e * (dp[b] - at["delta"][b])
            pair_ref[n, b] = ds.astype(jnp.bfloat16)
            acc_ref[b] = ds if n == 0 else acc_ref[b] + ds

    def multiply(n, at):
        dq = tdot(pair_ref[n, 0:128], kv_ref[n, 0:16], 1, 1)
        at["out"] = jnp.where(left, dq, at["attn"]).T.astype(jnp.bfloat16)
        lhs = jnp.concatenate([at["q"], at["scaled"].astype(jnp.float32).T], 1)
        at["grad"] = tdot(lhs.astype(jnp.bfloat16), pair_ref[n], 1, 0).astype(jnp.bfloat16)

    stages = [score, exponentiate, attend, differentiate, multiply]
    for step in range(8 + len(stages) - 1):
        for lag, stage in enumerate(stages):
            if 0 <= step - lag < 8:
                stage(step - lag, state[step - lag])
    outs, grads = [at["out"] for at in state], [at["grad"] for at in state]
    for dl in range(4):
        for zl in range(2):
            part = slice(zl * 64, zl * 64 + 64)
            oq_ref[zl * 4 + dl] = jnp.concatenate([outs[dl * 2 + s][:, part] for s in range(2)], 1)
            for y in range(8):
                r = zl * 8 + y
                part_y = slice(r * 64, r * 64 + 64)
                dkv_ref[PEER[y], zl * 4 + dl] = jnp.concatenate(
                    [grads[dl * 2 + s][:, part_y] for s in range(2)], 1
                )


def join_kernel(keep_ref, got_ref, out_ref):
    for x in range(4):
        for h in range(HEADS):
            both = keep_ref[x, h].astype(jnp.float32) + got_ref[x, h].astype(jnp.float32)
            out_ref[x, h] = both.astype(jnp.bfloat16)


def total(blocks):
    acc = blocks[0].astype(jnp.float32)
    for block in blocks[1:]:
        acc += block.astype(jnp.float32)
    return acc.astype(jnp.bfloat16)


def sum_kernel(oq_ref, dkv_ref, db_ref, pack_ref):
    for h in range(HEADS):
        pack_ref[h, 0:16] = oq_ref[h]
        pack_ref[h, 16:32] = total([dkv_ref[y, h] for y in range(8)])
        pack_ref[h, 32:48] = total([db_ref[x, h] for x in range(4)])


def finish_kernel(pack_ref, save_ref, wm_ref, wf_ref, up_ref, dx_ref, db_ref):
    dq, dk, dv, attn = [], [], [], []
    for h in range(HEADS):
        own = pack_ref[h].astype(jnp.float32)
        dq.append(own[0:8] * SCALE)
        attn.append(own[8:16])
        dk.append(own[16:24])
        dv.append(own[24:32])
        for r in range(2):
            db_ref[h, r : r + 1] = jnp.concatenate(
                [own[32 + r * 8 + c : 33 + r * 8 + c] for c in range(8)], 1
            )
    attn = jnp.concatenate(attn, 0)
    xhat, g, d_gated, rstd = save_ref[0:64], save_ref[64:128], save_ref[128:192], save_ref[192:193]
    gated = (g * attn).astype(jnp.bfloat16)
    up_ref[...] = tdot(gated, wf_ref[...], 0, 0).astype(jnp.bfloat16)
    d_gate = d_gated * attn * g * (1.0 - g)
    d_proj = jnp.concatenate(dq + dk + dv + [d_gate], 0).astype(jnp.bfloat16)
    d_normed = tdot(wm_ref[...], d_proj, 1, 0)
    dx = rstd * (
        d_normed
        - jnp.mean(d_normed, 0, keepdims=True)
        - xhat * jnp.mean(d_normed * xhat, 0, keepdims=True)
    )
    dx_ref[...] = dx.T.astype(jnp.bfloat16)


def call(kernel, outs, *args, scratch=(), space=pltpu.VMEM, limit=40):
    return pl.pallas_call(
        kernel,
        out_shape=outs,
        in_specs=[pl.BlockSpec(memory_space=space)] * len(args),
        out_specs=[pl.BlockSpec(memory_space=pltpu.VMEM)] * len(outs),
        scratch_shapes=list(scratch),
        compiler_params=pltpu.CompilerParams(vmem_limit_bytes=limit * 1024 * 1024),
    )(*args)


def shape(*dims, dtype=jnp.bfloat16):
    return jax.ShapeDtypeStruct(dims, dtype)


def exchange(a, axes):
    return lax.all_to_all(a, axes, 0, 0, tiled=True)


def swap_core(a):
    return lax.ppermute(a, "core", [(0, 1), (1, 0)])


def per_device(x, bias, wm, wf, rc):
    f32 = jnp.float32
    pack, saved = call(
        project_kernel,
        [shape(8, 48, 128), shape(200, 128, dtype=f32)],
        x.reshape(128, 64), rc.reshape(128, 64), wm, wf, bias,
        scratch=[pltpu.VMEM((128, 64), jnp.bfloat16), pltpu.VMEM((128, 64), jnp.bfloat16),
                 pltpu.VMEM((64, 256), jnp.bfloat16), pltpu.VMEM((64, 64), jnp.bfloat16),
                 pltpu.VMEM((8, 2, 1024), jnp.bfloat16), pltpu.SemaphoreType.DMA((5,))],
        space=pltpu.HBM, limit=60,
    )
    pack = exchange(pack, HEAD_AXES)
    rows = pack[:, 32:48]
    rows = exchange(jnp.broadcast_to(rows[None], (4,) + rows.shape), ("x",))
    own = jnp.broadcast_to(pack[None, :, 16:32], (8, 8, 16, 128))
    own, rows = lax.optimization_barrier((own, rows))
    kv = exchange(own, KEY_AXES)
    layout = [pltpu.VMEM((8, 8, 16, 128), f32), pltpu.VMEM((8, 128, 128), f32)]
    (bias_rows,) = call(bias_kernel, [shape(128, 1024, dtype=f32)], rows, swap_core(rows), scratch=layout)
    block, quad, octet = shape(8, 16, 128), shape(4, 8, 16, 128), shape(8, 8, 16, 128)
    oq, dkv, acc = call(
        attend_kernel,
        [block, octet, shape(128, 1024, dtype=f32)],
        pack, kv, bias_rows,
        scratch=[pltpu.VMEM((8, 32, 1024), jnp.bfloat16), pltpu.VMEM((8, 128, 1024), f32),
                 pltpu.VMEM((8, 256, 1024), jnp.bfloat16)],
    )
    dkv = exchange(dkv, KEY_AXES)
    keep, give = call(bias_grad_kernel, [quad, quad], acc, scratch=layout)
    (db,) = call(join_kernel, [quad], keep, swap_core(give))
    dkv, db = lax.optimization_barrier((dkv, db))
    db = exchange(db, ("x",))
    (back,) = call(sum_kernel, [shape(8, 48, 128)], oq, dkv, db)
    back = exchange(back, HEAD_AXES)
    update, dx, d_bias = call(
        finish_kernel,
        [shape(128, 64), shape(128, 64), shape(8, 2, 1024, dtype=f32)],
        back, saved, wm, wf,
    )
    return update.reshape(2, 64, 64), dx.reshape(2, 64, 64), d_bias


def solution(mesh):
    fine = Mesh(mesh.devices.reshape(4, 4, 2, 2, 2, 4), DEPTH + RES)
    tokens = P(DEPTH, RES, None)
    rows = P(None, RES + DEPTH, None)
    return jax.shard_map(
        per_device,
        mesh=fine,
        in_specs=(tokens, rows, P(), P(), tokens),
        out_specs=(tokens, tokens, rows),
        check_vma=False,
    )
```

```python
import math

import jax
import jax.numpy as jnp
from jax import lax
from jax.experimental import pallas as pl
from jax.experimental.pallas import tpu as pltpu
from jax.sharding import Mesh, PartitionSpec as P

HEADS = 8
PEER = [i % 4 * 2 + i // 4 for i in range(8)]
SOURCE = [[PEER[zh * 2 + zl] for zh in range(4)] for zl in range(2)]
HEAD_DIM = 8
EPS = 1e-05
SCALE = 1.0 / math.sqrt(HEAD_DIM)

DEPTH = ("x", "zhh", "zhl", "core")
RES = ("zl", "yh", "yl")
HEAD_AXES = ("zhl", "zl", "zhh")
KEY_AXES = ("yl", "yh")


def tdot(a, b, ca, cb):
    return lax.dot_general(a, b, (((ca,), (cb,)), ((), ())), preferred_element_type=jnp.float32)


def project_kernel(x_hbm, rc_hbm, wm_hbm, wf_hbm, bias_hbm, pack_ref, save_ref,
                   x_ref, rc_ref, wm_ref, wf_ref, bias_ref, sems):
    pairs = [(x_hbm, x_ref), (wm_hbm, wm_ref), (rc_hbm, rc_ref), (wf_hbm, wf_ref), (bias_hbm, bias_ref)]
    copies = [pltpu.make_async_copy(a, b, sems.at[i]) for i, (a, b) in enumerate(pairs)]
    for copy in copies:
        copy.start()
    for copy in copies:
        copy.wait()
    x = x_ref[...].astype(jnp.float32).T
    cent = x - jnp.mean(x, 0, keepdims=True)
    rstd = lax.rsqrt(jnp.mean(cent * cent, 0, keepdims=True) + EPS)
    xhat = cent * rstd
    proj = tdot(wm_ref[...], xhat.astype(jnp.bfloat16), 0, 0)
    g = jax.nn.sigmoid(proj[192:256])
    d_gated = tdot(wf_ref[...], rc_ref[...], 1, 1)
    d_attn = d_gated * g
    save_ref[...] = jnp.concatenate([xhat, g, d_gated, jnp.broadcast_to(rstd, (8, 128))], 0)
    for h in range(HEADS):
        lo, hi = h * HEAD_DIM, (h + 1) * HEAD_DIM
        b = bias_ref[h].astype(jnp.float32)
        parts = [proj[lo:hi] * SCALE, d_attn[lo:hi], proj[64 + lo : 64 + hi], proj[128 + lo : 128 + hi]]
        parts += [b[r : r + 1, c * 128 : c * 128 + 128] for r in range(2) for c in range(8)]
        pack_ref[h] = jnp.concatenate(parts, 0).astype(jnp.bfloat16)


GROUPS = [(zl, x) for zl in range(2) for x in range(4)]


def bias_kernel(own_ref, sibling_ref, bias_ref, wide_ref, tmp_ref):
    core = lax.axis_index("core")
    for x in range(4):
        for h in range(8):
            wide_ref[x * 2 + core, h] = own_ref[x, h].astype(jnp.float32)
            wide_ref[x * 2 + 1 - core, h] = sibling_ref[x, h].astype(jnp.float32)
    for i, (zl, x) in enumerate(GROUPS):
        for zh in range(4):
            for half in range(2):
                at = (zh * 2 + half) * 16
                tmp_ref[i, at : at + 16] = wide_ref[x * 2 + half, SOURCE[zl][zh]]
    for i in range(8):
        for c in range(8):
            bias_ref[i * 16 : i * 16 + 16, c * 128 : c * 128 + 128] = tmp_ref[i, pl.ds(c, 16, stride=8)]


def bias_grad_kernel(acc_ref, keep_ref, give_ref, wide_ref, tmp_ref):
    core = lax.axis_index("core")
    for i in range(8):
        for c in range(8):
            tmp_ref[i, pl.ds(c, 16, stride=8)] = acc_ref[i * 16 : i * 16 + 16, c * 128 : c * 128 + 128]
    for i, (zl, x) in enumerate(GROUPS):
        for zh in range(4):
            for half in range(2):
                at = (zh * 2 + half) * 16
                wide_ref[x * 2 + half, SOURCE[zl][zh]] = tmp_ref[i, at : at + 16]
    for x in range(4):
        for h in range(8):
            keep_ref[x, h] = wide_ref[x * 2 + core, h].astype(jnp.bfloat16)
            give_ref[x, h] = wide_ref[x * 2 + 1 - core, h].astype(jnp.bfloat16)


def attend_kernel(pack_ref, kv_in_ref, bias_ref, oq_ref, dkv_ref, acc_ref, kv_ref, t_ref, pair_ref):
    left = lax.broadcasted_iota(jnp.int32, (128, 16), 1) < HEAD_DIM
    blocks = [slice(at, at + 16) for at in range(0, 128, 16)]
    upper = lax.broadcasted_iota(jnp.int32, (16, 128), 0) < HEAD_DIM
    state = [{} for n in range(8)]
    ones = jnp.ones((16, 1024), jnp.bfloat16)

    def score(n, at):
        dl, lanes = n // 2, slice(n % 2 * 64, n % 2 * 64 + 64)
        kv_ref[n, 0:16] = jnp.concatenate(
            [kv_in_ref[PEER[y], SOURCE[zl][dl]][:, lanes] for zl in range(2) for y in range(8)], 1
        )
        kv_ref[n, 16:32] = ones
        qd = jnp.concatenate([pack_ref[SOURCE[zl][dl], 0:16][:, lanes] for zl in range(2)], 1)
        qd = qd.astype(jnp.float32)
        rows = qd.T
        q = jnp.where(left, rows, 0.0).astype(jnp.bfloat16)
        at["q"], at["d"] = jnp.where(upper, qd, 0.0), jnp.where(left, 0.0, rows)
        scores = tdot(q, kv_ref[n, 0:16], 1, 0)
        at["top"] = []
        for b in blocks:
            t = scores[b] + bias_ref[b]
            t_ref[n, b] = t
            at["top"].append(jnp.max(t, 1, keepdims=True))

    def exponentiate(n, at):
        for i, b in enumerate(blocks):
            e = jnp.exp(t_ref[n, b] - at["top"][i])
            pair_ref[n, 128 + i * 16 : 144 + i * 16] = e.astype(jnp.bfloat16)

    def attend(n, at):
        summed = tdot(pair_ref[n, 128:256], kv_ref[n], 1, 1)
        inverse = 1.0 / summed[:, 16:32]
        at["attn"] = summed[:, 0:16] * inverse
        at["scaled"] = (at["d"] * inverse).astype(jnp.bfloat16)
        at["delta"] = jnp.sum(at["scaled"].astype(jnp.float32) * at["attn"], 1, keepdims=True)

    def differentiate(n, at):
        dp = tdot(at["scaled"], kv_ref[n, 0:16], 1, 0)
        for i, b in enumerate(blocks):
            e = pair_ref[n, 128 + i * 16 : 144 + i * 16].astype(jnp.float32)
            ds = e * (dp[b] - at["delta"][b])
            pair_ref[n, b] = ds.astype(jnp.bfloat16)
            acc_ref[b] = ds if n == 0 else acc_ref[b] + ds

    def multiply(n, at):
        dq = tdot(pair_ref[n, 0:128], kv_ref[n, 0:16], 1, 1)
        at["out"] = jnp.where(left, dq, at["attn"]).T.astype(jnp.bfloat16)
        lhs = jnp.concatenate([at["q"], at["scaled"].astype(jnp.float32).T], 1)
        at["grad"] = tdot(lhs.astype(jnp.bfloat16), pair_ref[n], 1, 0).astype(jnp.bfloat16)

    stages = [score, exponentiate, attend, differentiate, multiply]
    for step in range(8 + len(stages) - 1):
        for lag, stage in enumerate(stages):
            if 0 <= step - lag < 8:
                stage(step - lag, state[step - lag])
    outs, grads = [at["out"] for at in state], [at["grad"] for at in state]
    for dl in range(4):
        for zl in range(2):
            part = slice(zl * 64, zl * 64 + 64)
            oq_ref[SOURCE[zl][dl]] = jnp.concatenate([outs[dl * 2 + s][:, part] for s in range(2)], 1)
            for y in range(8):
                r = zl * 8 + y
                part_y = slice(r * 64, r * 64 + 64)
                dkv_ref[PEER[y], SOURCE[zl][dl]] = jnp.concatenate(
                    [grads[dl * 2 + s][:, part_y] for s in range(2)], 1
                )


def join_kernel(keep_ref, got_ref, out_ref):
    for x in range(4):
        for h in range(HEADS):
            both = keep_ref[x, h].astype(jnp.float32) + got_ref[x, h].astype(jnp.float32)
            out_ref[x, h] = both.astype(jnp.bfloat16)


def total(blocks):
    acc = blocks[0].astype(jnp.float32)
    for block in blocks[1:]:
        acc += block.astype(jnp.float32)
    return acc.astype(jnp.bfloat16)


def sum_kernel(oq_ref, dkv_ref, db_ref, pack_ref):
    for h in range(HEADS):
        pack_ref[h, 0:16] = oq_ref[h]
        pack_ref[h, 16:32] = total([dkv_ref[y, h] for y in range(8)])
        pack_ref[h, 32:48] = total([db_ref[x, h] for x in range(4)])


def finish_kernel(pack_ref, save_ref, wm_ref, wf_ref, up_ref, dx_ref, db_ref):
    dq, dk, dv, attn = [], [], [], []
    for h in range(HEADS):
        own = pack_ref[h].astype(jnp.float32)
        dq.append(own[0:8] * SCALE)
        attn.append(own[8:16])
        dk.append(own[16:24])
        dv.append(own[24:32])
        for r in range(2):
            db_ref[h, r : r + 1] = jnp.concatenate(
                [own[32 + r * 8 + c : 33 + r * 8 + c] for c in range(8)], 1
            )
    attn = jnp.concatenate(attn, 0)
    xhat, g, d_gated, rstd = save_ref[0:64], save_ref[64:128], save_ref[128:192], save_ref[192:193]
    gated = (g * attn).astype(jnp.bfloat16)
    up_ref[...] = tdot(gated, wf_ref[...], 0, 0).astype(jnp.bfloat16)
    d_gate = d_gated * attn * g * (1.0 - g)
    d_proj = jnp.concatenate(dq + dk + dv + [d_gate], 0).astype(jnp.bfloat16)
    d_normed = tdot(wm_ref[...], d_proj, 1, 0)
    dx = rstd * (
        d_normed
        - jnp.mean(d_normed, 0, keepdims=True)
        - xhat * jnp.mean(d_normed * xhat, 0, keepdims=True)
    )
    dx_ref[...] = dx.T.astype(jnp.bfloat16)


def call(kernel, outs, *args, scratch=(), space=pltpu.VMEM, limit=40):
    return pl.pallas_call(
        kernel,
        out_shape=outs,
        in_specs=[pl.BlockSpec(memory_space=space)] * len(args),
        out_specs=[pl.BlockSpec(memory_space=pltpu.VMEM)] * len(outs),
        scratch_shapes=list(scratch),
        compiler_params=pltpu.CompilerParams(vmem_limit_bytes=limit * 1024 * 1024),
    )(*args)


def shape(*dims, dtype=jnp.bfloat16):
    return jax.ShapeDtypeStruct(dims, dtype)


def exchange(a, axes):
    return lax.all_to_all(a, axes, 0, 0, tiled=True)


def swap_core(a):
    return lax.ppermute(a, "core", [(0, 1), (1, 0)])


def per_device(x, bias, wm, wf, rc):
    f32 = jnp.float32
    pack, saved = call(
        project_kernel,
        [shape(8, 48, 128), shape(200, 128, dtype=f32)],
        x.reshape(128, 64), rc.reshape(128, 64), wm, wf, bias,
        scratch=[pltpu.VMEM((128, 64), jnp.bfloat16), pltpu.VMEM((128, 64), jnp.bfloat16),
                 pltpu.VMEM((64, 256), jnp.bfloat16), pltpu.VMEM((64, 64), jnp.bfloat16),
                 pltpu.VMEM((8, 2, 1024), jnp.bfloat16), pltpu.SemaphoreType.DMA((5,))],
        space=pltpu.HBM, limit=60,
    )
    pack = exchange(pack, HEAD_AXES)
    rows = pack[:, 32:48]
    rows = exchange(jnp.broadcast_to(rows[None], (4,) + rows.shape), ("x",))
    own = jnp.broadcast_to(pack[None, :, 16:32], (8, 8, 16, 128))
    own, rows = lax.optimization_barrier((own, rows))
    kv = exchange(own, KEY_AXES)
    layout = [pltpu.VMEM((8, 8, 16, 128), f32), pltpu.VMEM((8, 128, 128), f32)]
    (bias_rows,) = call(bias_kernel, [shape(128, 1024, dtype=f32)], rows, swap_core(rows), scratch=layout)
    block, quad, octet = shape(8, 16, 128), shape(4, 8, 16, 128), shape(8, 8, 16, 128)
    oq, dkv, acc = call(
        attend_kernel,
        [block, octet, shape(128, 1024, dtype=f32)],
        pack, kv, bias_rows,
        scratch=[pltpu.VMEM((8, 32, 1024), jnp.bfloat16), pltpu.VMEM((8, 128, 1024), f32),
                 pltpu.VMEM((8, 256, 1024), jnp.bfloat16)],
    )
    dkv = exchange(dkv, KEY_AXES)
    keep, give = call(bias_grad_kernel, [quad, quad], acc, scratch=layout)
    (db,) = call(join_kernel, [quad], keep, swap_core(give))
    dkv, db = lax.optimization_barrier((dkv, db))
    db = exchange(db, ("x",))
    (back,) = call(sum_kernel, [shape(8, 48, 128)], oq, dkv, db)
    back = exchange(back, HEAD_AXES)
    update, dx, d_bias = call(
        finish_kernel,
        [shape(128, 64), shape(128, 64), shape(8, 2, 1024, dtype=f32)],
        back, saved, wm, wf,
    )
    return update.reshape(2, 64, 64), dx.reshape(2, 64, 64), d_bias


def solution(mesh):
    fine = Mesh(mesh.devices.reshape(4, 2, 2, 2, 2, 2, 4), DEPTH + RES)
    tokens = P(DEPTH, RES, None)
    rows = P(None, RES + DEPTH, None)
    return jax.shard_map(
        per_device,
        mesh=fine,
        in_specs=(tokens, rows, P(), P(), tokens),
        out_specs=(tokens, tokens, rows),
        check_vma=False,
    )
```

```python
import math

import jax
import jax.numpy as jnp
from jax import lax
from jax.experimental import pallas as pl
from jax.experimental.pallas import tpu as pltpu
from jax.sharding import Mesh, PartitionSpec as P

HEADS = 8
PEER = [i % 4 * 2 + i // 4 for i in range(8)]
SOURCE = [[PEER[zh * 2 + zl] for zh in range(4)] for zl in range(2)]
HEAD_DIM = 8
EPS = 1e-05
SCALE = 1.0 / math.sqrt(HEAD_DIM)

DEPTH = ("x", "zhh", "zhl", "core")
RES = ("zl", "y")
HEAD_AXES = ("zhl", "zl", "zhh")
RING = [i * 3 % 8 for i in range(8)]


def tdot(a, b, ca, cb):
    return lax.dot_general(a, b, (((ca,), (cb,)), ((), ())), preferred_element_type=jnp.float32)


def project_kernel(x_hbm, rc_hbm, wm_hbm, wf_hbm, bias_hbm, pack_ref, save_ref,
                   x_ref, rc_ref, wm_ref, wf_ref, bias_ref, sems):
    pairs = [(x_hbm, x_ref), (wm_hbm, wm_ref), (rc_hbm, rc_ref), (wf_hbm, wf_ref), (bias_hbm, bias_ref)]
    copies = [pltpu.make_async_copy(a, b, sems.at[i]) for i, (a, b) in enumerate(pairs)]
    for copy in copies:
        copy.start()
    for copy in copies:
        copy.wait()
    x = x_ref[...].astype(jnp.float32).T
    cent = x - jnp.mean(x, 0, keepdims=True)
    rstd = lax.rsqrt(jnp.mean(cent * cent, 0, keepdims=True) + EPS)
    xhat = cent * rstd
    proj = tdot(wm_ref[...], xhat.astype(jnp.bfloat16), 0, 0)
    g = jax.nn.sigmoid(proj[192:256])
    d_gated = tdot(wf_ref[...], rc_ref[...], 1, 1)
    d_attn = d_gated * g
    save_ref[...] = jnp.concatenate([xhat, g, d_gated, jnp.broadcast_to(rstd, (8, 128))], 0)
    for h in range(HEADS):
        lo, hi = h * HEAD_DIM, (h + 1) * HEAD_DIM
        b = bias_ref[h].astype(jnp.float32)
        parts = [proj[lo:hi] * SCALE, d_attn[lo:hi], proj[64 + lo : 64 + hi], proj[128 + lo : 128 + hi]]
        parts += [b[r : r + 1, c * 128 : c * 128 + 128] for r in range(2) for c in range(8)]
        pack_ref[h] = jnp.concatenate(parts, 0).astype(jnp.bfloat16)


GROUPS = [(zl, x) for zl in range(2) for x in range(4)]


def bias_kernel(own_ref, sibling_ref, bias_ref, wide_ref, tmp_ref):
    core = lax.axis_index("core")
    for x in range(4):
        for h in range(8):
            wide_ref[x * 2 + core, h] = own_ref[x, h].astype(jnp.float32)
            wide_ref[x * 2 + 1 - core, h] = sibling_ref[x, h].astype(jnp.float32)
    for i, (zl, x) in enumerate(GROUPS):
        for zh in range(4):
            for half in range(2):
                at = (zh * 2 + half) * 16
                tmp_ref[i, at : at + 16] = wide_ref[x * 2 + half, SOURCE[zl][zh]]
    for i in range(8):
        for c in range(8):
            bias_ref[i * 16 : i * 16 + 16, c * 128 : c * 128 + 128] = tmp_ref[i, pl.ds(c, 16, stride=8)]


def bias_grad_kernel(acc_ref, keep_ref, give_ref, wide_ref, tmp_ref):
    core = lax.axis_index("core")
    for i in range(8):
        for c in range(8):
            tmp_ref[i, pl.ds(c, 16, stride=8)] = acc_ref[i * 16 : i * 16 + 16, c * 128 : c * 128 + 128]
    for i, (zl, x) in enumerate(GROUPS):
        for zh in range(4):
            for half in range(2):
                at = (zh * 2 + half) * 16
                wide_ref[x * 2 + half, SOURCE[zl][zh]] = tmp_ref[i, at : at + 16]
    for x in range(4):
        for h in range(8):
            keep_ref[x, h] = wide_ref[x * 2 + core, h].astype(jnp.bfloat16)
            give_ref[x, h] = wide_ref[x * 2 + 1 - core, h].astype(jnp.bfloat16)


def attend_kernel(pack_ref, kv_in_ref, bias_ref, oq_ref, dkv_ref, acc_ref, kv_ref, t_ref, pair_ref):
    left = lax.broadcasted_iota(jnp.int32, (128, 16), 1) < HEAD_DIM
    blocks = [slice(at, at + 16) for at in range(0, 128, 16)]
    upper = lax.broadcasted_iota(jnp.int32, (16, 128), 0) < HEAD_DIM
    state = [{} for n in range(8)]
    ones = jnp.ones((16, 1024), jnp.bfloat16)

    def score(n, at):
        dl, lanes = n // 2, slice(n % 2 * 64, n % 2 * 64 + 64)
        kv_ref[n, 0:16] = jnp.concatenate(
            [kv_in_ref[RING[y], SOURCE[zl][dl]][:, lanes] for zl in range(2) for y in range(8)], 1
        )
        kv_ref[n, 16:32] = ones
        qd = jnp.concatenate([pack_ref[SOURCE[zl][dl], 0:16][:, lanes] for zl in range(2)], 1)
        qd = qd.astype(jnp.float32)
        rows = qd.T
        q = jnp.where(left, rows, 0.0).astype(jnp.bfloat16)
        at["q"], at["d"] = jnp.where(upper, qd, 0.0), jnp.where(left, 0.0, rows)
        scores = tdot(q, kv_ref[n, 0:16], 1, 0)
        at["top"] = []
        for b in blocks:
            t = scores[b] + bias_ref[b]
            t_ref[n, b] = t
            at["top"].append(jnp.max(t, 1, keepdims=True))

    def exponentiate(n, at):
        for i, b in enumerate(blocks):
            e = jnp.exp(t_ref[n, b] - at["top"][i])
            pair_ref[n, 128 + i * 16 : 144 + i * 16] = e.astype(jnp.bfloat16)

    def attend(n, at):
        summed = tdot(pair_ref[n, 128:256], kv_ref[n], 1, 1)
        inverse = 1.0 / summed[:, 16:32]
        at["attn"] = summed[:, 0:16] * inverse
        at["scaled"] = (at["d"] * inverse).astype(jnp.bfloat16)
        at["delta"] = jnp.sum(at["scaled"].astype(jnp.float32) * at["attn"], 1, keepdims=True)

    def differentiate(n, at):
        dp = tdot(at["scaled"], kv_ref[n, 0:16], 1, 0)
        for i, b in enumerate(blocks):
            e = pair_ref[n, 128 + i * 16 : 144 + i * 16].astype(jnp.float32)
            ds = e * (dp[b] - at["delta"][b])
            pair_ref[n, b] = ds.astype(jnp.bfloat16)
            acc_ref[b] = ds if n == 0 else acc_ref[b] + ds

    def multiply(n, at):
        dq = tdot(pair_ref[n, 0:128], kv_ref[n, 0:16], 1, 1)
        at["out"] = jnp.where(left, dq, at["attn"]).T.astype(jnp.bfloat16)
        lhs = jnp.concatenate([at["q"], at["scaled"].astype(jnp.float32).T], 1)
        at["grad"] = tdot(lhs.astype(jnp.bfloat16), pair_ref[n], 1, 0).astype(jnp.bfloat16)

    stages = [score, exponentiate, attend, differentiate, multiply]
    for step in range(8 + len(stages) - 1):
        for lag, stage in enumerate(stages):
            if 0 <= step - lag < 8:
                stage(step - lag, state[step - lag])
    outs, grads = [at["out"] for at in state], [at["grad"] for at in state]
    for dl in range(4):
        for zl in range(2):
            part = slice(zl * 64, zl * 64 + 64)
            oq_ref[SOURCE[zl][dl]] = jnp.concatenate([outs[dl * 2 + s][:, part] for s in range(2)], 1)
            for y in range(8):
                r = zl * 8 + y
                part_y = slice(r * 64, r * 64 + 64)
                dkv_ref[RING[y], SOURCE[zl][dl]] = jnp.concatenate(
                    [grads[dl * 2 + s][:, part_y] for s in range(2)], 1
                )


def join_kernel(keep_ref, got_ref, out_ref):
    for x in range(4):
        for h in range(HEADS):
            both = keep_ref[x, h].astype(jnp.float32) + got_ref[x, h].astype(jnp.float32)
            out_ref[x, h] = both.astype(jnp.bfloat16)


def total(blocks):
    acc = blocks[0].astype(jnp.float32)
    for block in blocks[1:]:
        acc += block.astype(jnp.float32)
    return acc.astype(jnp.bfloat16)


def sum_kernel(oq_ref, dkv_ref, db_ref, pack_ref):
    for h in range(HEADS):
        pack_ref[h, 0:16] = oq_ref[h]
        pack_ref[h, 16:32] = total([dkv_ref[y, h] for y in range(8)])
        pack_ref[h, 32:48] = total([db_ref[x, h] for x in range(4)])


def finish_kernel(pack_ref, save_ref, wm_ref, wf_ref, up_ref, dx_ref, db_ref):
    dq, dk, dv, attn = [], [], [], []
    for h in range(HEADS):
        own = pack_ref[h].astype(jnp.float32)
        dq.append(own[0:8] * SCALE)
        attn.append(own[8:16])
        dk.append(own[16:24])
        dv.append(own[24:32])
        for r in range(2):
            db_ref[h, r : r + 1] = jnp.concatenate(
                [own[32 + r * 8 + c : 33 + r * 8 + c] for c in range(8)], 1
            )
    attn = jnp.concatenate(attn, 0)
    xhat, g, d_gated, rstd = save_ref[0:64], save_ref[64:128], save_ref[128:192], save_ref[192:193]
    gated = (g * attn).astype(jnp.bfloat16)
    up_ref[...] = tdot(gated, wf_ref[...], 0, 0).astype(jnp.bfloat16)
    d_gate = d_gated * attn * g * (1.0 - g)
    d_proj = jnp.concatenate(dq + dk + dv + [d_gate], 0).astype(jnp.bfloat16)
    d_normed = tdot(wm_ref[...], d_proj, 1, 0)
    dx = rstd * (
        d_normed
        - jnp.mean(d_normed, 0, keepdims=True)
        - xhat * jnp.mean(d_normed * xhat, 0, keepdims=True)
    )
    dx_ref[...] = dx.T.astype(jnp.bfloat16)


def call(kernel, outs, *args, scratch=(), space=pltpu.VMEM, limit=40):
    return pl.pallas_call(
        kernel,
        out_shape=outs,
        in_specs=[pl.BlockSpec(memory_space=space)] * len(args),
        out_specs=[pl.BlockSpec(memory_space=pltpu.VMEM)] * len(outs),
        scratch_shapes=list(scratch),
        compiler_params=pltpu.CompilerParams(vmem_limit_bytes=limit * 1024 * 1024),
    )(*args)


def shape(*dims, dtype=jnp.bfloat16):
    return jax.ShapeDtypeStruct(dims, dtype)


def exchange(a, axes, groups=None):
    return lax.all_to_all(a, axes, 0, 0, axis_index_groups=groups, tiled=True)


def swap_core(a):
    return lax.ppermute(a, "core", [(0, 1), (1, 0)])


def per_device(x, bias, wm, wf, rc):
    f32 = jnp.float32
    pack, saved = call(
        project_kernel,
        [shape(8, 48, 128), shape(200, 128, dtype=f32)],
        x.reshape(128, 64), rc.reshape(128, 64), wm, wf, bias,
        scratch=[pltpu.VMEM((128, 64), jnp.bfloat16), pltpu.VMEM((128, 64), jnp.bfloat16),
                 pltpu.VMEM((64, 256), jnp.bfloat16), pltpu.VMEM((64, 64), jnp.bfloat16),
                 pltpu.VMEM((8, 2, 1024), jnp.bfloat16), pltpu.SemaphoreType.DMA((5,))],
        space=pltpu.HBM, limit=60,
    )
    pack = exchange(pack, HEAD_AXES)
    rows = pack[:, 32:48]
    rows = exchange(jnp.broadcast_to(rows[None], (4,) + rows.shape), ("x",))
    own = jnp.broadcast_to(pack[None, :, 16:32], (8, 8, 16, 128))
    own, rows = lax.optimization_barrier((own, rows))
    kv = exchange(own, "y", [RING])
    layout = [pltpu.VMEM((8, 8, 16, 128), f32), pltpu.VMEM((8, 128, 128), f32)]
    (bias_rows,) = call(bias_kernel, [shape(128, 1024, dtype=f32)], rows, swap_core(rows), scratch=layout)
    block, quad, octet = shape(8, 16, 128), shape(4, 8, 16, 128), shape(8, 8, 16, 128)
    oq, dkv, acc = call(
        attend_kernel,
        [block, octet, shape(128, 1024, dtype=f32)],
        pack, kv, bias_rows,
        scratch=[pltpu.VMEM((8, 32, 1024), jnp.bfloat16), pltpu.VMEM((8, 128, 1024), f32),
                 pltpu.VMEM((8, 256, 1024), jnp.bfloat16)],
    )
    dkv = exchange(dkv, "y", [RING])
    keep, give = call(bias_grad_kernel, [quad, quad], acc, scratch=layout)
    (db,) = call(join_kernel, [quad], keep, swap_core(give))
    dkv, db = lax.optimization_barrier((dkv, db))
    db = exchange(db, ("x",))
    (back,) = call(sum_kernel, [shape(8, 48, 128)], oq, dkv, db)
    back = exchange(back, HEAD_AXES)
    update, dx, d_bias = call(
        finish_kernel,
        [shape(128, 64), shape(128, 64), shape(8, 2, 1024, dtype=f32)],
        back, saved, wm, wf,
    )
    return update.reshape(2, 64, 64), dx.reshape(2, 64, 64), d_bias


def solution(mesh):
    fine = Mesh(mesh.devices.reshape(4, 2, 2, 2, 2, 8), DEPTH + RES)
    tokens = P(DEPTH, RES, None)
    rows = P(None, RES + DEPTH, None)
    return jax.shard_map(
        per_device,
        mesh=fine,
        in_specs=(tokens, rows, P(), P(), tokens),
        out_specs=(tokens, tokens, rows),
        check_vma=False,
    )
```
